256 devices in a mesh: section: 2 (over y_lo), blk: 128 (over y_hi, x, z, core).
Axes of the slice: x: 4, y: 4 (y_hi: 2, y_lo: 2; y = y_hi * 2 + y_lo), z: 8, core: 2. Of those that a mesh axis runs over, the one named last changes fastest.
Arguments:
- traces: bfloat16 [8, 4096, 6144], P('section', 'blk'), may hold values from -8 to 8
- counts: int32 [128], P('blk'), may hold values from 1 to 32, 2560 in all
- taps: float32 [64], replicated, may hold values from -0.75 to 0.75
- masks: int32 [6], replicated, may hold values from 1 to 127, as said below
Outputs:
- cross: bfloat16 [128, 6, 2, 32, 32, 768], P('blk', None, None, None, None, 'section')
The draws below stay inside these ranges and needn't reach their ends.
Inputs may be any that keep to these rules, and one draw needn't show every extreme that they name: The first counts[b] slots of block b hold its live channels; the counts sum to 2560. The masks are distinct; one round pairs block b with block 127 - b, and one with block b XOR 1.
All inputs are finite; a program needn't handle non-finite values.
Results may differ from the reference program's by a relative error of at most 0.0067.
Values may be sent and summed in bfloat16 or wider, within the bound.
No kernel may reach another device: no remote copies, remote signals or barrier semaphores. Data moves between devices by JAX's collectives and lax.ppermute only.
A program may use at most 128 MiB of HBM per device.

```python
import math
import jax
import jax.numpy as jnp
import numpy as np
from jax import lax

L = 6144
F = 768
K = 64
CAP = 32
SEG = 8
CHANNELS = 4096
ROUNDS = 6
N_BLK = 128


def draw_masks(key, part):
    key = jax.random.fold_in(key, 7)
    first, second = jax.random.split(key)
    others = jax.random.permutation(first, N_BLK - 3)[:ROUNDS - 2].astype(jnp.int32) + 2
    values = jnp.concatenate([jnp.array([N_BLK - 1, 1], jnp.int32), others])
    order = jax.random.permutation(second, ROUNDS)
    return values[order]


def level_of(rng, shape, shards, smallest, top_value):
    factor_of = 1.0
    for axis_at, blocks in shards:
        steps = jax.random.uniform(jax.random.fold_in(jax.random.fold_in(rng, 6), axis_at), (blocks,), jnp.float32, smallest / len(shards), top_value / len(shards))
        factor_of = factor_of * jnp.repeat(jnp.exp(steps), shape[axis_at] // blocks).reshape((-1,) + (1,) * (len(shape) - 1 - axis_at))
    return factor_of


def profile(amount, total, reach, lean):
    portions = [(1 << 20) // math.isqrt(grade ** lean) + 1 for grade in range(2, amount + 1)]
    spare, holding = total - reach - (amount - 1), [1] * (amount - 1)
    while spare > 0:
        movable = [i for i in range(amount - 1) if holding[i] < reach]
        mass, left = sum([portions[i] for i in movable]), spare
        for i in movable:
            more = min(reach - holding[i], max(1, left * portions[i] // mass), spare)
            holding[i] = holding[i] + more
            spare = spare - more
    return np.array([reach] + holding)


def uneven_parts(own_key, number_of, total, most, lean):
    if number_of == 2:
        one = jax.random.randint(own_key, (), max(1, total - most), min(most, total - 1) + 1)
        return jnp.stack([one, total - one])
    tallies = jnp.asarray(profile(number_of, total, most, lean), jnp.int32)
    twos = (number_of - 1) // 2
    donor, taker = tallies[1:1 + 2 * twos:2], tallies[2:2 + 2 * twos:2]
    margin = jnp.minimum(donor - 1, most - taker)
    moved = jax.random.randint(jax.random.fold_in(own_key, 1), (twos,), 0, 1 << 20) % (margin + 1)
    tallies = tallies.at[1:1 + 2 * twos:2].set(donor - moved).at[2:2 + 2 * twos:2].set(taker + moved)
    return tallies[jax.random.permutation(jax.random.fold_in(own_key, 2), number_of)]


def centred(rng, extent, width, most, pieces=(), held_as=jnp.bfloat16):
    factor_of = level_of(rng, extent, pieces, -0.22, 0.18) if pieces else 1.0
    values = jax.random.normal(rng, extent, jnp.float32) * width * factor_of
    return jnp.minimum(jnp.maximum(values, -most), most).astype(held_as)


def setup_inputs(seed: int = 0) -> dict:
    streams_of = jax.random.split(jax.random.key(seed), 5)
    traces = centred(streams_of[0], (SEG, CHANNELS, L), 1.0, 8.0, ((0, 2), (1, 128)))
    counts = uneven_parts(streams_of[1], N_BLK, 5 * CAP * N_BLK // 8, CAP, 2).astype(jnp.int32)
    taps = centred(streams_of[2], (K,), K ** -0.5, 0.75, (), jnp.float32)
    masks = draw_masks(jax.random.fold_in(streams_of[4], 71), 0)
    return {"traces": traces, "counts": counts, "taps": taps, "masks": masks}


def dft_table(start, count, length):
    times = jnp.arange(count, dtype=jnp.int32) + start
    freqs = jnp.arange(F, dtype=jnp.int32)
    phase = times[:, None] * freqs[None, :] % length
    angle = phase.astype(jnp.float32) * (2.0 * math.pi / length)
    return jnp.concatenate([jnp.cos(angle), -jnp.sin(angle)], axis=1).astype(jnp.bfloat16)

def response(taps, length):
    steps = jnp.arange(taps.shape[0], dtype=jnp.int32)
    freqs = jnp.arange(F, dtype=jnp.int32)
    phase = steps[:, None] * freqs[None, :] % length
    angle = phase.astype(jnp.float32) * (2.0 * math.pi / length)
    real = jnp.dot(taps, jnp.cos(angle), precision=lax.Precision.HIGHEST)
    imag = -jnp.dot(taps, jnp.sin(angle), precision=lax.Precision.HIGHEST)
    return (real, imag)

def clip_rows(signal):
    values = signal.astype(jnp.float32)
    level = jnp.sqrt(lax.optimization_barrier(jnp.mean(values * values, axis=1, keepdims=True)) + 1e-06)
    return jnp.clip(values, -2.5 * level, 2.5 * level).astype(jnp.bfloat16)

def whiten(spectrum, live, real_resp, imag_resp):
    real_part = spectrum[:, :F]
    imag_part = spectrum[:, F:]
    filt_re = real_part * real_resp - imag_part * imag_resp
    filt_im = real_part * imag_resp + imag_part * real_resp
    power = lax.optimization_barrier(jnp.mean(filt_re * filt_re + filt_im * filt_im, axis=1, keepdims=True)) + 1e-06
    scale = live[:, None] / jnp.sqrt(power)
    return jnp.stack([filt_re * scale, filt_im * scale], axis=1).astype(jnp.bfloat16)

def correlate_ref(own, partner, segments):
    other = jnp.concatenate([own[:, :, 1:2], -own[:, :, 0:1]], axis=2)
    left = jnp.stack([own, other]).astype(jnp.float32)
    right = partner.astype(jnp.float32)
    total = jnp.einsum('asikf,sjkf->aijf', left, right)
    return (total * (1.0 / segments)).astype(jnp.bfloat16)

def reference(traces, counts, taps, masks):
    table = dft_table(0, L, L)
    real_resp, imag_resp = response(taps, L)
    slots = jnp.arange(CAP, dtype=jnp.int32)
    live = (slots[None, :] < counts[:, None]).reshape(-1).astype(jnp.float32)

    def one_segment(signal):
        clipped = clip_rows(signal)
        spectrum = jnp.dot(clipped, table, preferred_element_type=jnp.float32)
        return whiten(spectrum, live, real_resp, imag_resp)
    spectra = lax.map(one_segment, traces)
    spectra = spectra.reshape(SEG, N_BLK, CAP, 2, F)

    def one_block(block):
        own = lax.dynamic_index_in_dim(spectra, block, 1, keepdims=False)
        results = []
        for rnd in range(ROUNDS):
            mate = jnp.bitwise_xor(block, masks[rnd]).astype(jnp.int32)
            partner = lax.dynamic_index_in_dim(spectra, mate, 1, keepdims=False)
            results.append(correlate_ref(own, partner, SEG))
        return jnp.stack(results)
    return lax.map(one_block, jnp.arange(N_BLK, dtype=jnp.int32))
```

```python
import jax
import jax.numpy as jnp
import numpy as np
from jax import lax
from jax.experimental import pallas as pl
from jax.experimental.pallas import tpu as pltpu
from jax.sharding import Mesh
from jax.sharding import PartitionSpec as P

F = 768
L = 6144
K = 64
CAP = 32
SEG = 8
ROUNDS = 6
LOCAL = 4
HALF = F // 2
Q = L // 4
G = 256
CLASSES = (0, 2, 1, 3)
VMEM = 48 * 1024 * 1024


def angles(steps, freqs):
    return (np.outer(steps, freqs) % L) * (2.0 * np.pi / L)


def class_bins(residue):
    return 4 * np.arange(F // 4) + residue


def dft_tables():
    out = np.zeros((4, Q, 2 * G), np.float32)
    for at, residue in enumerate(CLASSES):
        angle = angles(np.arange(Q), class_bins(residue))
        out[at, :, : F // 4] = np.cos(angle)
        out[at, :, G : G + F // 4] = np.sin(angle)
    return out.astype(jnp.bfloat16)


def tap_tables():
    out = np.zeros((2, K, 4 * G), np.float32)
    for at, residue in enumerate(CLASSES):
        angle = angles(np.arange(K), class_bins(residue))
        out[0, :, at * G : at * G + F // 4] = np.cos(angle)
        out[1, :, at * G : at * G + F // 4] = np.sin(angle)
    return out


def spectra_kernel(counts, x, taps, tap_table, table, out, y, re, im):
    step = pl.program_id(0)
    rows = x.shape[0]

    @pl.when(step == 0)
    def _():
        def tile(t, carry):
            at = pl.ds(pl.multiple_of(t * 16, 16), 16)
            total = jnp.zeros((16, 128), jnp.float32)
            for c in range(L // 128):
                v = x[at, c * 128 : (c + 1) * 128].astype(jnp.float32)
                total = total + v * v
            mean = jnp.sum(total, axis=1, keepdims=True) * (1.0 / L)
            top = jnp.broadcast_to(2.5 * jnp.sqrt(mean + 1e-6), (16, 128))

            def clipped(start):
                v = x[at, start : start + 128].astype(jnp.float32)
                v = jnp.minimum(jnp.maximum(v, -top), top)
                return v.astype(jnp.bfloat16).astype(jnp.float32)

            for c in range(Q // 128):
                x0, x1, x2, x3 = [clipped(q * Q + c * 128) for q in range(4)]
                s02, d02, s13, d13 = x0 + x2, x0 - x2, x1 + x3, x1 - x3
                for n, v in enumerate((s02 + s13, s02 - s13, d02, -d13)):
                    hi = v.astype(jnp.bfloat16)
                    lo = (v - hi.astype(jnp.float32)).astype(jnp.bfloat16)
                    y[2 * n, at, c * 128 : (c + 1) * 128] = hi
                    y[2 * n + 1, at, c * 128 : (c + 1) * 128] = lo
            return carry

        lax.fori_loop(0, rows // 16, tile, 0)

    def product(n):
        a = jnp.dot(y[2 * n], table[0], preferred_element_type=jnp.float32)
        b = jnp.dot(y[2 * n + 1], table[0], preferred_element_type=jnp.float32)
        return a + b

    for at in range(2):

        @pl.when(step == at)
        def _(at=at):
            s = product(at)
            re[:, at * G : (at + 1) * G] = s[:, :G]
            im[:, at * G : (at + 1) * G] = -s[:, G:]

    for at in range(2, 4):

        @pl.when(step == at)
        def _(at=at):
            p, q = product(2), product(3)
            if at == 2:
                re[:, at * G : (at + 1) * G] = p[:, :G] + q[:, G:]
                im[:, at * G : (at + 1) * G] = q[:, :G] - p[:, G:]
            else:
                re[:, at * G : (at + 1) * G] = p[:, :G] - q[:, G:]
                im[:, at * G : (at + 1) * G] = -(p[:, G:] + q[:, :G])

    @pl.when(step == 3)
    def _():
        hr = jnp.sum(tap_table[0] * taps[...], axis=0, keepdims=True)
        hi = -jnp.sum(tap_table[1] * taps[...], axis=0, keepdims=True)
        fr = re[...] * hr - im[...] * hi
        fi = re[...] * hi + im[...] * hr
        power = jnp.sum(fr * fr + fi * fi, axis=1, keepdims=True) * (1.0 / F) + 1e-6
        slot = lax.broadcasted_iota(jnp.int32, (rows, 1), 0) % CAP
        live = jnp.where(slot < counts[0], 1.0, 0.0)
        scale = live / jnp.sqrt(power)
        white = jnp.concatenate([fr * scale, fi * scale], axis=0).astype(jnp.bfloat16)
        src = lax.broadcasted_iota(jnp.int32, (4 * G, F), 0)
        dst = lax.broadcasted_iota(jnp.int32, (4 * G, F), 1)
        residue = dst % 4
        place = jnp.where(residue == 1, 2, jnp.where(residue == 2, 1, residue))
        spread = jnp.where(src == place * G + dst // 4, 1.0, 0.0).astype(jnp.bfloat16)
        ordered = jnp.dot(white, spread, preferred_element_type=jnp.float32).astype(jnp.bfloat16)
        for half in range(2):
            for seg in range(LOCAL):
                for part in range(2):
                    start = part * rows + seg * CAP
                    out[half, seg * 2 + part] = ordered[start : start + CAP, half * HALF : (half + 1) * HALF]


def spectra_of(traces, counts, taps):
    segs, cap, length = traces.shape
    rows = segs * cap
    return pl.pallas_call(
        spectra_kernel,
        out_shape=jax.ShapeDtypeStruct((2, 2 * segs, cap, HALF), jnp.bfloat16),
        grid=(4,),
        in_specs=[
            pl.BlockSpec(memory_space=pltpu.SMEM),
            pl.BlockSpec((rows, length), lambda i: (0, 0)),
            pl.BlockSpec((K, 1), lambda i: (0, 0)),
            pl.BlockSpec((2, K, 4 * G), lambda i: (0, 0, 0)),
            pl.BlockSpec((1, Q, 2 * G), lambda i: (i, 0, 0)),
        ],
        out_specs=pl.BlockSpec((2, 2 * segs, cap, HALF), lambda i: (0, 0, 0, 0)),
        scratch_shapes=[
            pltpu.VMEM((8, rows, Q), jnp.bfloat16),
            pltpu.VMEM((rows, 4 * G), jnp.float32),
            pltpu.VMEM((rows, 4 * G), jnp.float32),
        ],
        compiler_params=pltpu.CompilerParams(vmem_limit_bytes=VMEM),
        name="spectra",
    )(counts, traces.reshape(rows, length), taps.reshape(K, 1), tap_tables(), dft_tables())


def pick_kernel(place, gathered, out, sems):
    copies = []
    for d in range(out.shape[0]):
        for r in range(out.shape[1]):
            copies.append(
                pltpu.make_async_copy(
                    gathered.at[place[0, r], :, jnp.bitwise_xor(place[1, r], d)],
                    out.at[d, r],
                    sems.at[d * out.shape[1] + r],
                )
            )
    for copy in copies:
        copy.start()
    for copy in copies:
        copy.wait()


def pick(gathered, place, rounds):
    return pl.pallas_call(
        pick_kernel,
        out_shape=jax.ShapeDtypeStruct((8, rounds, 2, CAP, HALF), jnp.bfloat16),
        in_specs=[pl.BlockSpec(memory_space=pltpu.SMEM), pl.BlockSpec(memory_space=pl.ANY)],
        out_specs=pl.BlockSpec(memory_space=pl.ANY),
        scratch_shapes=[pltpu.SemaphoreType.DMA((8 * rounds,))],
        name="pick",
    )(place, gathered)


def cross_kernel(info, mine, other, partner, kept, out, left):
    @pl.when(pl.program_id(0) == 0)
    def _():
        for where, block in ((info[0], mine), (1 - info[0], other)):
            for seg in range(LOCAL):
                a_re = block[0, 2 * seg].astype(jnp.float32) * (1.0 / SEG)
                a_im = block[0, 2 * seg + 1].astype(jnp.float32) * (1.0 / SEG)
                for n, v in enumerate((a_re + a_im, a_re, a_im)):
                    left[n * SEG + where * LOCAL + seg] = v

    def tile(at, carry):
        lanes = pl.ds(pl.multiple_of(at // 2 * 128, 128), 128)
        rows = pl.ds(pl.multiple_of(at % 2 * 16, 16), 16)
        b1, b2, b3 = [], [], []
        for sec in range(2):
            for seg in range(LOCAL):
                b_re = partner[2 * seg, 0, sec, rows, lanes].astype(jnp.float32)
                b_im = partner[2 * seg + 1, 0, sec, rows, lanes].astype(jnp.float32)
                b1.append(b_re)
                b2.append(b_re + b_im)
                b3.append(b_im - b_re)
        for i in range(CAP):
            k1 = k2 = k3 = None
            for s in range(SEG):
                t1 = left[s, i : i + 1, lanes] * b1[s]
                t2 = left[SEG + s, i : i + 1, lanes] * b2[s]
                t3 = left[2 * SEG + s, i : i + 1, lanes] * b3[s]
                k1 = t1 if k1 is None else k1 + t1
                k2 = t2 if k2 is None else k2 + t2
                k3 = t3 if k3 is None else k3 + t3
            out[0, 0, i, rows, lanes] = (k1 + k3).astype(jnp.bfloat16)
            out[0, 1, i, rows, lanes] = (k1 - k2).astype(jnp.bfloat16)
        return carry

    lax.fori_loop(0, HALF // 128 * (CAP // 16), tile, 0)


def cross_of(info, own, other, partner, kept):
    rounds = partner.shape[1]
    out = jax.ShapeDtypeStruct((ROUNDS, 2, CAP, CAP, HALF), jnp.bfloat16)
    block = (2 * LOCAL, CAP, HALF)
    fresh = kept is None
    in_specs = [
        pl.BlockSpec((1,) + block, lambda r, info: (info[0], 0, 0, 0)),
        pl.BlockSpec((1,) + block, lambda r, info: (0, 0, 0, 0)),
        pl.BlockSpec((2 * LOCAL, 1, 2, CAP, HALF), lambda r, info: (0, r, 0, 0, 0)),
    ]
    args = [own, other, partner]
    if not fresh:
        in_specs.append(pl.BlockSpec(memory_space=pl.ANY))
        args.append(kept)

    def kernel(info_ref, mine_ref, other_ref, partner_ref, *rest):
        cross_kernel(info_ref, mine_ref, other_ref, partner_ref, None, rest[-2], rest[-1])

    return pl.pallas_call(
        kernel,
        out_shape=out,
        grid_spec=pltpu.PrefetchScalarGridSpec(
            num_scalar_prefetch=1,
            grid=(rounds,),
            in_specs=in_specs,
            out_specs=pl.BlockSpec((1, 2, CAP, CAP, HALF), lambda r, info: (info[1 + r], 0, 0, 0, 0)),
            scratch_shapes=[pltpu.VMEM((3 * SEG, CAP, HALF), jnp.float32)],
        ),
        input_output_aliases={} if fresh else {4: 0},
        compiler_params=pltpu.CompilerParams(vmem_limit_bytes=VMEM),
        cost_estimate=pl.CostEstimate(flops=rounds * 8 * SEG * CAP * CAP * HALF, bytes_accessed=rounds * 2000000, transcendentals=0),
        name="cross",
    )(info, *args)


def shards(traces, counts, taps, masks):
    section = lax.axis_index("section")
    zcore = lax.axis_index("z") * 2 + lax.axis_index("core")
    near = jnp.argmax(masks == 1).astype(jnp.int32)
    far = jnp.arange(ROUNDS - 1, dtype=jnp.int32)
    far = far + (far >= near).astype(jnp.int32)
    far_masks = masks[far]

    white = spectra_of(traces, counts, taps)
    pieces = lax.all_to_all(white.reshape(16, CAP, HALF), ("section", "yh", "x"), 0, 0, tiled=True)
    gathered = lax.all_gather(pieces, ("z", "core"), axis=0, tiled=False)

    own = lax.dynamic_index_in_dim(white, section, 0, keepdims=True)
    away = lax.dynamic_index_in_dim(white, 1 - section, 0, keepdims=True)
    other = lax.ppermute(away, "section", [(0, 1), (1, 0)])
    both = jnp.where(section == 0, jnp.stack([own[0], other[0]], 1), jnp.stack([other[0], own[0]], 1))
    sibling = lax.ppermute(both, "core", [(0, 1), (1, 0)])
    first = cross_of(jnp.stack([section, near]), white, other, sibling[:, None], None)

    place = jnp.stack([jnp.bitwise_xor(zcore, far_masks & 15), far_masks >> 4])
    picked = pick(gathered.reshape(16, 2, 8, CAP, HALF), place, ROUNDS - 1)
    partners = lax.all_to_all(picked, ("yh", "x"), 0, 0, tiled=True)
    result = cross_of(jnp.concatenate([section[None], far]), white, other, partners, first)
    return result[None]


def solution(mesh):
    fine = Mesh(mesh.devices.reshape(2, 2, 4, 8, 2), ("section", "yh", "x", "z", "core"))
    blk = ("yh", "x", "z", "core")
    return jax.shard_map(
        shards,
        mesh=fine,
        in_specs=(P("section", blk, None), P(blk), P(), P()),
        out_specs=P(blk, None, None, None, None, "section"),
        check_vma=False,
    )
```

```python
import jax
import jax.numpy as jnp
import numpy as np
from jax import lax
from jax.experimental import pallas as pl
from jax.experimental.pallas import tpu as pltpu
from jax.sharding import Mesh
from jax.sharding import PartitionSpec as P

F = 768
L = 6144
K = 64
CAP = 32
SEG = 8
ROUNDS = 6
LOCAL = 4
HALF = F // 2
Q = L // 4
G = 256
CLASSES = (0, 2, 1, 3)
VMEM = 48 * 1024 * 1024


def angles(steps, freqs):
    return (np.outer(steps, freqs) % L) * (2.0 * np.pi / L)


def class_bins(residue):
    return 4 * np.arange(F // 4) + residue


def dft_tables():
    out = np.zeros((4, Q, 2 * G), np.float32)
    for at, residue in enumerate(CLASSES):
        angle = angles(np.arange(Q), class_bins(residue))
        out[at, :, : F // 4] = np.cos(angle)
        out[at, :, G : G + F // 4] = np.sin(angle)
    return out.astype(jnp.bfloat16)


def tap_tables():
    out = np.zeros((2, K, 4 * G), np.float32)
    for at, residue in enumerate(CLASSES):
        angle = angles(np.arange(K), class_bins(residue))
        out[0, :, at * G : at * G + F // 4] = np.cos(angle)
        out[1, :, at * G : at * G + F // 4] = np.sin(angle)
    return out


def spectra_kernel(counts, x, taps, tap_table, table, out, y, re, im):
    step = pl.program_id(0)
    rows = x.shape[0]

    @pl.when(step == 0)
    def _():
        def tile(t, carry):
            at = pl.ds(pl.multiple_of(t * 16, 16), 16)
            total = jnp.zeros((16, 128), jnp.float32)
            for c in range(L // 128):
                v = x[at, c * 128 : (c + 1) * 128].astype(jnp.float32)
                total = total + v * v
            mean = jnp.sum(total, axis=1, keepdims=True) * (1.0 / L)
            top = jnp.broadcast_to(2.5 * jnp.sqrt(mean + 1e-6), (16, 128))

            def clipped(start):
                v = x[at, start : start + 128].astype(jnp.float32)
                v = jnp.minimum(jnp.maximum(v, -top), top)
                return v.astype(jnp.bfloat16).astype(jnp.float32)

            for c in range(Q // 128):
                x0, x1, x2, x3 = [clipped(q * Q + c * 128) for q in range(4)]
                s02, d02, s13, d13 = x0 + x2, x0 - x2, x1 + x3, x1 - x3
                for n, v in enumerate((s02 + s13, s02 - s13, d02, -d13)):
                    hi = v.astype(jnp.bfloat16)
                    lo = (v - hi.astype(jnp.float32)).astype(jnp.bfloat16)
                    y[2 * n, at, c * 128 : (c + 1) * 128] = hi
                    y[2 * n + 1, at, c * 128 : (c + 1) * 128] = lo
            return carry

        lax.fori_loop(0, rows // 16, tile, 0)

    def product(n):
        a = jnp.dot(y[2 * n], table[0], preferred_element_type=jnp.float32)
        b = jnp.dot(y[2 * n + 1], table[0], preferred_element_type=jnp.float32)
        return a + b

    for at in range(2):

        @pl.when(step == at)
        def _(at=at):
            s = product(at)
            re[:, at * G : (at + 1) * G] = s[:, :G]
            im[:, at * G : (at + 1) * G] = -s[:, G:]

    for at in range(2, 4):

        @pl.when(step == at)
        def _(at=at):
            p, q = product(2), product(3)
            if at == 2:
                re[:, at * G : (at + 1) * G] = p[:, :G] + q[:, G:]
                im[:, at * G : (at + 1) * G] = q[:, :G] - p[:, G:]
            else:
                re[:, at * G : (at + 1) * G] = p[:, :G] - q[:, G:]
                im[:, at * G : (at + 1) * G] = -(p[:, G:] + q[:, :G])

    @pl.when(step == 3)
    def _():
        hr = jnp.sum(tap_table[0] * taps[...], axis=0, keepdims=True)
        hi = -jnp.sum(tap_table[1] * taps[...], axis=0, keepdims=True)
        fr = re[...] * hr - im[...] * hi
        fi = re[...] * hi + im[...] * hr
        power = jnp.sum(fr * fr + fi * fi, axis=1, keepdims=True) * (1.0 / F) + 1e-6
        slot = lax.broadcasted_iota(jnp.int32, (rows, 1), 0) % CAP
        live = jnp.where(slot < counts[0], 1.0, 0.0)
        scale = live / jnp.sqrt(power)
        white = jnp.concatenate([fr * scale, fi * scale], axis=0).astype(jnp.bfloat16)
        src = lax.broadcasted_iota(jnp.int32, (4 * G, F), 0)
        dst = lax.broadcasted_iota(jnp.int32, (4 * G, F), 1)
        residue = dst % 4
        place = jnp.where(residue == 1, 2, jnp.where(residue == 2, 1, residue))
        spread = jnp.where(src == place * G + dst // 4, 1.0, 0.0).astype(jnp.bfloat16)
        ordered = jnp.dot(white, spread, preferred_element_type=jnp.float32).astype(jnp.bfloat16)
        for half in range(2):
            for seg in range(LOCAL):
                for part in range(2):
                    start = part * rows + seg * CAP
                    out[half, seg * 2 + part] = ordered[start : start + CAP, half * HALF : (half + 1) * HALF]


def spectra_of(traces, counts, taps):
    segs, cap, length = traces.shape
    rows = segs * cap
    return pl.pallas_call(
        spectra_kernel,
        out_shape=jax.ShapeDtypeStruct((2, 2 * segs, cap, HALF), jnp.bfloat16),
        grid=(4,),
        in_specs=[
            pl.BlockSpec(memory_space=pltpu.SMEM),
            pl.BlockSpec((rows, length), lambda i: (0, 0)),
            pl.BlockSpec((K, 1), lambda i: (0, 0)),
            pl.BlockSpec((2, K, 4 * G), lambda i: (0, 0, 0)),
            pl.BlockSpec((1, Q, 2 * G), lambda i: (i, 0, 0)),
        ],
        out_specs=pl.BlockSpec((2, 2 * segs, cap, HALF), lambda i: (0, 0, 0, 0)),
        scratch_shapes=[
            pltpu.VMEM((8, rows, Q), jnp.bfloat16),
            pltpu.VMEM((rows, 4 * G), jnp.float32),
            pltpu.VMEM((rows, 4 * G), jnp.float32),
        ],
        compiler_params=pltpu.CompilerParams(vmem_limit_bytes=VMEM),
        name="spectra",
    )(counts, traces.reshape(rows, length), taps.reshape(K, 1), tap_tables(), dft_tables())


def pick_kernel(place, gathered, out, sems):
    copies = []
    for d in range(out.shape[0]):
        for r in range(out.shape[1]):
            copies.append(
                pltpu.make_async_copy(
                    gathered.at[place[0, r], :, jnp.bitwise_xor(place[1, r], d)],
                    out.at[d, r],
                    sems.at[d * out.shape[1] + r],
                )
            )
    for copy in copies:
        copy.start()
    for copy in copies:
        copy.wait()


def pick(gathered, place):
    rounds = place.shape[1]
    return pl.pallas_call(
        pick_kernel,
        out_shape=jax.ShapeDtypeStruct((8, rounds, 2, CAP, HALF), jnp.bfloat16),
        in_specs=[pl.BlockSpec(memory_space=pltpu.SMEM), pl.BlockSpec(memory_space=pl.ANY)],
        out_specs=pl.BlockSpec(memory_space=pltpu.VMEM),
        scratch_shapes=[pltpu.SemaphoreType.DMA((8 * rounds,))],
        compiler_params=pltpu.CompilerParams(vmem_limit_bytes=VMEM),
        name="pick",
    )(place, gathered)


def products(left, right, n, lo, rows, lanes):
    sums = [None] * 8
    for s in range(n * SEG, (n + 1) * SEG):
        b = right[s, rows, lanes]
        for i in range(8):
            t = left[s, lo + i : lo + i + 1, lanes] * b
            sums[i] = t if sums[i] is None else sums[i] + t
    return sums


def cross_kernel(order, own, partner, out, left, right, by_piece):
    @pl.when(pl.program_id(0) == 0)
    def _():
        for s in range(SEG):
            sec, seg = divmod(s, LOCAL)
            a_re = own[sec, 2 * seg].astype(jnp.float32) * (1.0 / SEG)
            a_im = own[sec, 2 * seg + 1].astype(jnp.float32) * (1.0 / SEG)
            left[s] = a_re + a_im
            left[SEG + s] = a_re
            left[2 * SEG + s] = a_im

    for s in range(SEG):
        sec, seg = divmod(s, LOCAL)
        if by_piece:
            b_re, b_im = partner[2 * seg, 0, sec], partner[2 * seg + 1, 0, sec]
        else:
            b_re, b_im = partner[sec, 2 * seg], partner[sec, 2 * seg + 1]
        b_re, b_im = b_re.astype(jnp.float32), b_im.astype(jnp.float32)
        right[s] = b_re
        right[SEG + s] = b_re + b_im
        right[2 * SEG + s] = b_im - b_re

    def tile(at, carry):
        lanes = pl.ds(pl.multiple_of(at // 2 * 128, 128), 128)
        rows = pl.ds(pl.multiple_of(at % 2 * 16, 16), 16)
        for lo in range(0, CAP, 8):
            k1 = products(left, right, 0, lo, rows, lanes)
            k3 = products(left, right, 2, lo, rows, lanes)
            for i in range(8):
                out[0, 0, lo + i, rows, lanes] = (k1[i] + k3[i]).astype(jnp.bfloat16)
            k2 = products(left, right, 1, lo, rows, lanes)
            for i in range(8):
                out[0, 1, lo + i, rows, lanes] = (k1[i] - k2[i]).astype(jnp.bfloat16)
        return carry

    lax.fori_loop(0, HALF // 128 * (CAP // 16), tile, 0)


def cross_of(order, own, partner, kept):
    rounds = order.shape[0]
    by_piece = partner.ndim == 5
    half = (2, 2 * LOCAL, CAP, HALF)
    in_specs = [
        pl.BlockSpec(half, lambda r, order: (0, 0, 0, 0)),
        pl.BlockSpec((2 * LOCAL, 1, 2, CAP, HALF), lambda r, order: (0, r, 0, 0, 0))
        if by_piece
        else pl.BlockSpec(half, lambda r, order: (0, 0, 0, 0)),
    ]
    args = [own, partner]
    if kept is not None:
        in_specs.append(pl.BlockSpec(memory_space=pl.ANY))
        args.append(kept)

    def kernel(order_ref, own_ref, partner_ref, *rest):
        cross_kernel(order_ref, own_ref, partner_ref, *rest[-3:], by_piece)

    return pl.pallas_call(
        kernel,
        out_shape=jax.ShapeDtypeStruct((ROUNDS, 2, CAP, CAP, HALF), jnp.bfloat16),
        grid_spec=pltpu.PrefetchScalarGridSpec(
            num_scalar_prefetch=1,
            grid=(rounds,),
            in_specs=in_specs,
            out_specs=pl.BlockSpec((1, 2, CAP, CAP, HALF), lambda r, order: (order[r], 0, 0, 0, 0)),
            scratch_shapes=[
                pltpu.VMEM((3 * SEG, CAP, HALF), jnp.float32),
                pltpu.VMEM((3 * SEG, CAP, HALF), jnp.float32),
            ],
        ),
        input_output_aliases={} if kept is None else {3: 0},
        compiler_params=pltpu.CompilerParams(vmem_limit_bytes=VMEM),
        cost_estimate=pl.CostEstimate(
            flops=rounds * 8 * SEG * CAP * CAP * HALF, bytes_accessed=rounds * 2000000, transcendentals=0
        ),
        name="cross",
    )(order, *args)


def flipped(block, axes, sizes, mask):
    count = int(np.prod(sizes))
    return lax.ppermute(block, axes, [(i, i ^ mask) for i in range(count)])


def shards(traces, counts, taps, masks):
    section = lax.axis_index("section")
    zcore = lax.axis_index("z") * 2 + lax.axis_index("core")

    white = spectra_of(traces, counts, taps)
    pieces = lax.all_to_all(white.reshape(16, CAP, HALF), ("section", "yh", "x"), 0, 0, tiled=True)
    gathered = lax.all_gather(pieces, ("z", "core"), axis=0, tiled=False)

    white, _ = lax.optimization_barrier((white, pieces))
    own = lax.dynamic_index_in_dim(white, section, 0, keepdims=True)
    away = lax.dynamic_index_in_dim(white, 1 - section, 0, keepdims=True)
    other = flipped(away, "section", (2,), 1)
    both = jnp.where(section == 0, jnp.concatenate([own, other]), jnp.concatenate([other, own]))
    sibling = flipped(both, "core", (2,), 1)
    near = jnp.argmax(masks == 1).astype(jnp.int32)
    result = cross_of(near[None], both, sibling, None)

    far = jnp.arange(ROUNDS - 1, dtype=jnp.int32)
    far = far + (far >= near).astype(jnp.int32)
    far_masks = masks[far]
    place = jnp.stack([jnp.bitwise_xor(zcore, far_masks & 15), far_masks >> 4])
    gathered, result, place = lax.optimization_barrier((gathered, result, place))
    picked = pick(gathered.reshape(16, 2, 8, CAP, HALF), place)
    picked, far, both = lax.optimization_barrier((picked, far, both))
    partners = lax.all_to_all(picked, ("yh", "x"), 0, 0, tiled=True)
    return cross_of(far, both, partners, result)[None]


def solution(mesh):
    fine = Mesh(mesh.devices.reshape(2, 2, 4, 8, 2), ("section", "yh", "x", "z", "core"))
    blk = ("yh", "x", "z", "core")
    return jax.shard_map(
        shards,
        mesh=fine,
        in_specs=(P("section", blk, None), P(blk), P(), P()),
        out_specs=P(blk, None, None, None, None, "section"),
        check_vma=False,
    )
```

```python
import jax
import jax.numpy as jnp
import numpy as np
from jax import lax
from jax.experimental import pallas as pl
from jax.experimental.pallas import tpu as pltpu
from jax.sharding import Mesh
from jax.sharding import PartitionSpec as P

F = 768
L = 6144
K = 64
CAP = 32
SEG = 8
ROUNDS = 6
LOCAL = 4
HALF = F // 2
Q = L // 4
G = 256
CLASSES = (0, 2, 1, 3)
VMEM = 48 * 1024 * 1024


def angles(steps, freqs):
    return (np.outer(steps, freqs) % L) * (2.0 * np.pi / L)


def class_bins(residue):
    return 4 * np.arange(F // 4) + residue


def dft_tables():
    out = np.zeros((4, Q, 2 * G), np.float32)
    for at, residue in enumerate(CLASSES):
        angle = angles(np.arange(Q), class_bins(residue))
        out[at, :, : F // 4] = np.cos(angle)
        out[at, :, G : G + F // 4] = np.sin(angle)
    return out.astype(jnp.bfloat16)


def tap_tables():
    out = np.zeros((2, K, 4 * G), np.float32)
    for at, residue in enumerate(CLASSES):
        angle = angles(np.arange(K), class_bins(residue))
        out[0, :, at * G : at * G + F // 4] = np.cos(angle)
        out[1, :, at * G : at * G + F // 4] = np.sin(angle)
    return out


def spectra_kernel(counts, taps, traces, tap_source, table_source, out, x, tap_table, table, spread, y, re, im, sems):
    segs, rows = traces.shape[0], x.shape[0]
    loads = [pltpu.make_async_copy(traces.at[s], x.at[pl.ds(s * CAP, CAP)], sems.at[s]) for s in range(segs)]
    tables = [pltpu.make_async_copy(table_source.at[k], table.at[k], sems.at[segs + k]) for k in range(4)]
    tap_load = pltpu.make_async_copy(tap_source, tap_table, sems.at[segs + 4])
    for copy in loads + tables + [tap_load]:
        copy.start()

    src = lax.broadcasted_iota(jnp.int32, (4 * G, F), 0)
    dst = lax.broadcasted_iota(jnp.int32, (4 * G, F), 1)
    residue = dst & 3
    place = jnp.where(residue == 1, 2, jnp.where(residue == 2, 1, residue))
    spread[...] = jnp.where(src == place * G + (dst >> 2), 1.0, 0.0).astype(jnp.bfloat16)

    def tile(t, carry):
        at = pl.ds(pl.multiple_of(t * 16, 16), 16)
        total = jnp.zeros((16, 128), jnp.float32)
        for c in range(L // 128):
            v = x[at, c * 128 : (c + 1) * 128].astype(jnp.float32)
            total = total + v * v
        mean = jnp.sum(total, axis=1, keepdims=True) * (1.0 / L)
        top = jnp.broadcast_to(2.5 * jnp.sqrt(mean + 1e-6), (16, 128))

        def clipped(start):
            v = x[at, start : start + 128].astype(jnp.float32)
            v = jnp.minimum(jnp.maximum(v, -top), top)
            return v.astype(jnp.bfloat16).astype(jnp.float32)

        for c in range(Q // 128):
            x0, x1, x2, x3 = [clipped(q * Q + c * 128) for q in range(4)]
            s02, d02, s13, d13 = x0 + x2, x0 - x2, x1 + x3, x1 - x3
            for n, v in enumerate((s02 + s13, s02 - s13, d02, -d13)):
                hi = v.astype(jnp.bfloat16)
                lo = (v - hi.astype(jnp.float32)).astype(jnp.bfloat16)
                y[2 * n, at, c * 128 : (c + 1) * 128] = hi
                y[2 * n + 1, at, c * 128 : (c + 1) * 128] = lo
        return carry

    for s in range(segs):
        loads[s].wait()
        lax.fori_loop(s * CAP // 16, (s + 1) * CAP // 16, tile, 0)

    def product(n, k):
        a = jnp.dot(y[2 * n], table[k], preferred_element_type=jnp.float32)
        b = jnp.dot(y[2 * n + 1], table[k], preferred_element_type=jnp.float32)
        return a + b

    for k in range(4):
        tables[k].wait()
        at = slice(k * G, (k + 1) * G)
        if k < 2:
            p = product(k, k)
            re[:, at] = p[:, :G]
            im[:, at] = -p[:, G:]
        else:
            p, q = product(2, k), product(3, k)
            if k == 2:
                re[:, at] = p[:, :G] + q[:, G:]
                im[:, at] = q[:, :G] - p[:, G:]
            else:
                re[:, at] = p[:, :G] - q[:, G:]
                im[:, at] = -(p[:, G:] + q[:, :G])

    tap_load.wait()
    square = (K, K)
    same = lax.broadcasted_iota(jnp.int32, square, 0) == lax.broadcasted_iota(jnp.int32, square, 1)
    column = jnp.sum(jnp.where(same, jnp.broadcast_to(taps[...], square), 0.0), axis=1, keepdims=True)
    hr = jnp.sum(tap_table[0] * column, axis=0, keepdims=True)
    hi = -jnp.sum(tap_table[1] * column, axis=0, keepdims=True)
    fr = re[...] * hr - im[...] * hi
    fi = re[...] * hi + im[...] * hr
    power = jnp.sum(fr * fr + fi * fi, axis=1, keepdims=True) * (1.0 / F) + 1e-6
    slot = lax.broadcasted_iota(jnp.int32, (rows, 1), 0) % CAP
    live = jnp.where(slot < counts[0], 1.0, 0.0)
    scale = live / jnp.sqrt(power)
    white = jnp.concatenate([fr * scale, fi * scale], axis=0).astype(jnp.bfloat16)
    ordered = jnp.dot(white, spread[...], preferred_element_type=jnp.float32)
    for half in range(2):
        for seg in range(LOCAL):
            for part in range(2):
                start, piece = part * rows + seg * CAP, seg * 2 + part
                for fg in range(HALF // 128):
                    at = half * HALF + fg * 128
                    block = pltpu.roll(ordered[start : start + CAP, at : at + 128], 16 * piece, 1)
                    out[half, piece, :, fg * 128 : (fg + 1) * 128] = block.astype(jnp.bfloat16)


def spectra_of(traces, counts, taps):
    segs, cap, length = traces.shape
    rows = segs * cap
    far_away = pl.BlockSpec(memory_space=pl.ANY)
    return pl.pallas_call(
        spectra_kernel,
        out_shape=jax.ShapeDtypeStruct((2, 2 * segs, cap, HALF), jnp.bfloat16),
        in_specs=[
            pl.BlockSpec(memory_space=pltpu.SMEM),
            pl.BlockSpec(memory_space=pltpu.VMEM),
            far_away,
            far_away,
            far_away,
        ],
        out_specs=pl.BlockSpec(memory_space=pltpu.VMEM),
        scratch_shapes=[
            pltpu.VMEM((rows, length), jnp.bfloat16),
            pltpu.VMEM((2, K, 4 * G), jnp.float32),
            pltpu.VMEM((4, Q, 2 * G), jnp.bfloat16),
            pltpu.VMEM((4 * G, F), jnp.bfloat16),
            pltpu.VMEM((8, rows, Q), jnp.bfloat16),
            pltpu.VMEM((rows, 4 * G), jnp.float32),
            pltpu.VMEM((rows, 4 * G), jnp.float32),
            pltpu.SemaphoreType.DMA((segs + 5,)),
        ],
        compiler_params=pltpu.CompilerParams(vmem_limit_bytes=62 * 1024 * 1024),
        name="spectra",
    )(counts, taps.reshape(1, K), traces, tap_tables(), dft_tables())


def pick_kernel(place, *refs):
    slabs, out = (refs[:8], refs[8:16]), refs[16]
    for r in range(out.shape[1]):
        for k in range(8):

            @pl.when(place[0, r] == k)
            def _(r=r, k=k):
                for d in range(out.shape[0]):
                    src = jnp.bitwise_xor(place[1, r], d)
                    for h in range(2):
                        out[d, r, h] = slabs[h][k][src]


def pick(first, second, place):
    rounds = place.shape[1]
    inside = pl.BlockSpec(memory_space=pltpu.VMEM)
    return pl.pallas_call(
        pick_kernel,
        out_shape=jax.ShapeDtypeStruct((16, rounds, 2, CAP // 2, HALF), jnp.bfloat16),
        in_specs=[pl.BlockSpec(memory_space=pltpu.SMEM)] + [inside] * 16,
        out_specs=inside,
        compiler_params=pltpu.CompilerParams(vmem_limit_bytes=VMEM),
        name="pick",
    )(place, *first, *second)


def place_bits(shape, dtype):
    lane = lax.broadcasted_iota(dtype, shape, 1)
    return [(lane & (16 << b)) != 0 for b in range(3)]


def swirl(tiles, bits):
    held = [tiles[-n % 8] for n in range(8)]
    for b in range(3):
        held = [jnp.where(bits[b], held[(n - (1 << b)) % 8], held[n]) for n in range(8)]
    return held


def weights_kernel(own, out):
    bits = place_bits((8, 128), jnp.int32)
    row = lax.broadcasted_iota(jnp.int32, (16, 128), 0)
    diagonal = (lax.broadcasted_iota(jnp.int32, (16, 128), 1) & 15) == row
    for h in range(2):
        for piece in range(8):
            block = own[h, piece].astype(jnp.float32) * (1.0 / SEG)
            for tile in range(2):
                v = block[tile * 8 : (tile + 1) * 8]
                v = pltpu.roll(pltpu.roll(v, -16 * piece % 128, 1), 0, 1, stride=16, stride_axis=0)
                for b in range(3):
                    v = jnp.where(bits[b], pltpu.roll(v, 8 - (1 << b), 0), v)
                for g in range(8):
                    line = jnp.broadcast_to(v[-g % 8][None], (16, 128))
                    at = h * 128 + (g + piece) % 8 * 16
                    out[0, 0, g, at : at + 16, tile * 128 : (tile + 1) * 128] = jnp.where(
                        diagonal, line, 0.0
                    ).astype(jnp.bfloat16)


def weights_of(own):
    return pl.pallas_call(
        weights_kernel,
        out_shape=jax.ShapeDtypeStruct((HALF // 128, CAP // 16, 8, 256, 256), jnp.bfloat16),
        grid=(HALF // 128, CAP // 16),
        in_specs=[pl.BlockSpec((2, 8, 16, 128), lambda fg, it: (0, 0, it, fg))],
        out_specs=pl.BlockSpec((1, 1, 8, 256, 256), lambda fg, it: (fg, it, 0, 0, 0)),
        compiler_params=pltpu.CompilerParams(vmem_limit_bytes=VMEM),
        name="weights",
    )(own)


def cross_kernel(order, partner, sibling, weights, out, left, held, sums, done, load_sems, store_sems):
    bits = place_bits((16, 128), jnp.int16)
    groups, halves = HALF // 128, CAP // 16
    loads = [
        [pltpu.make_async_copy(weights.at[fg, it], held.at[fg, it], load_sems.at[fg * halves + it]) for it in range(halves)]
        for fg in range(groups)
    ]
    for it in range(halves):
        for fg in range(groups):
            loads[fg][it].start()

    def arrange(r, block):
        for fg in range(groups):
            for h in range(2):
                for jh in range(2):
                    x = [block(p, h, jh, slice(fg * 128, (fg + 1) * 128)) for p in range(8)]
                    turned = []
                    for p in range(8):
                        other = x[p ^ 1]
                        turned.append(pltpu.roll(other, 16, 1) if p % 2 else -pltpu.roll(other, 112, 1))
                    for a, tiles in enumerate((x, turned)):
                        at = pl.ds(pl.multiple_of((a * ROUNDS + r) * CAP + jh * 16, 16), 16)
                        for g, z in enumerate(swirl(tiles, bits)):
                            left[fg, g, at, h * 128 : (h + 1) * 128] = z

    def arrange_far(r, carry):
        arrange(r, lambda p, h, jh, lanes: partner[2 * p + jh, r, h, :, lanes])
        return carry

    lax.fori_loop(0, ROUNDS - 1, arrange_far, 0)
    arrange(ROUNDS - 1, lambda p, h, jh, lanes: sibling[h, p, jh * 16 : (jh + 1) * 16, lanes])

    def store(it, r):
        part = pl.ds(it * 16, 16)
        return pltpu.make_async_copy(done.at[r, :, part], out.at[order[r], :, part], store_sems.at[it * ROUNDS + r])

    for it in range(halves):
        for fg in range(groups):
            loads[fg][it].wait()
            for g in range(8):
                total = jnp.dot(left[fg, g], held[fg, it, g], preferred_element_type=jnp.float32)
                sums[fg, g] = total.astype(jnp.bfloat16)

        def finish(r, carry, it=it):
            for fg in range(groups):
                for a in range(2):
                    for jh in range(2):
                        rows = pl.ds(pl.multiple_of((a * ROUNDS + r) * CAP + jh * 16, 16), 16)
                        for tile in range(2):
                            cols = slice(tile * 128, (tile + 1) * 128)
                            turned = swirl([sums[fg, g, rows, cols] for g in range(8)], bits)
                            for i in range(8):
                                done[r, a, it * 16 + tile * 8 + i, jh * 16 : (jh + 1) * 16, fg * 128 : (fg + 1) * 128] = (
                                    pltpu.roll(turned[i], -16 * i % 128, 1)
                                )
            store(it, r).start()
            return carry

        lax.fori_loop(0, ROUNDS, finish, 0)

    for it in range(halves):
        for r in range(ROUNDS):
            store(it, r).wait()


def cross_of(order, partner, sibling, weights):
    rows = 2 * ROUNDS * CAP
    groups, halves = HALF // 128, CAP // 16
    shape = (ROUNDS, 2, CAP, CAP, HALF)
    return pl.pallas_call(
        cross_kernel,
        out_shape=jax.ShapeDtypeStruct(shape, jnp.bfloat16),
        in_specs=[
            pl.BlockSpec(memory_space=pltpu.SMEM),
            pl.BlockSpec(memory_space=pltpu.VMEM),
            pl.BlockSpec(memory_space=pltpu.VMEM),
            pl.BlockSpec(memory_space=pl.ANY),
        ],
        out_specs=pl.BlockSpec(memory_space=pl.ANY),
        scratch_shapes=[
            pltpu.VMEM((groups, 8, rows, 256), jnp.bfloat16),
            pltpu.VMEM((groups, halves, 8, 256, 256), jnp.bfloat16),
            pltpu.VMEM((groups, 8, rows, 256), jnp.bfloat16),
            pltpu.VMEM(shape, jnp.bfloat16),
            pltpu.SemaphoreType.DMA((groups * halves,)),
            pltpu.SemaphoreType.DMA((halves * ROUNDS,)),
        ],
        compiler_params=pltpu.CompilerParams(vmem_limit_bytes=VMEM),
        name="cross",
    )(order, partner, sibling, weights)


def flipped(block, axis):
    return lax.ppermute(block, axis, [(0, 1), (1, 0)])


def around(block, last):
    ring = lax.axis_size("z")

    def shift(held, way):
        return lax.ppermute(held, "z", [(i, (i + way) % ring) for i in range(ring)])

    slabs = [block] * ring
    for step in range(1, ring // 2):
        slabs[-step] = shift(slabs[1 - step], 1)
        slabs[step] = shift(slabs[step - 1], -1)
    slabs[ring // 2] = shift(slabs[(ring // 2 + last) % ring], last)
    return slabs


def shards(traces, counts, taps, masks):
    section = lax.axis_index("section")
    z = lax.axis_index("z")

    white = spectra_of(traces, counts, taps)
    pieces = lax.all_to_all(
        white.reshape(32, CAP // 2, HALF), ("section", "yh", "x", "core"), 0, 0, tiled=True
    )
    first, second = around(pieces[:16], 1), around(pieces[16:], -1)

    white, _ = lax.optimization_barrier((white, pieces))
    own = lax.dynamic_index_in_dim(white, section, 0, keepdims=True)
    away = lax.dynamic_index_in_dim(white, 1 - section, 0, keepdims=True)
    other = flipped(away, "section")
    both = jnp.where(section == 0, jnp.concatenate([own, other]), jnp.concatenate([other, own]))
    sibling = flipped(both, "core")
    weights = weights_of(both)
    near = jnp.argmax(masks == 1).astype(jnp.int32)
    far = jnp.arange(ROUNDS - 1, dtype=jnp.int32)
    far = far + (far >= near).astype(jnp.int32)
    far_masks = masks[far]
    order = jnp.concatenate([far, near[None]])
    apart = jnp.bitwise_xor(z, far_masks >> 1 & 7) - z & 7
    place = jnp.stack([apart, far_masks >> 4 << 1 | far_masks & 1])

    first, second, place, order, sibling, weights = lax.optimization_barrier(
        (first, second, place, order, sibling, weights)
    )
    picked = pick(first, second, place).reshape(16, -1, HALF)
    partners = lax.all_to_all(picked, ("yh", "x", "core"), 0, 0, tiled=True)
    partners = partners.reshape(16, ROUNDS - 1, 2, CAP // 2, HALF)
    return cross_of(order, partners, sibling, weights)[None]


def solution(mesh):
    fine = Mesh(mesh.devices.reshape(2, 2, 4, 8, 2), ("section", "yh", "x", "z", "core"))
    blk = ("yh", "x", "z", "core")
    return jax.shard_map(
        shards,
        mesh=fine,
        in_specs=(P("section", blk, None), P(blk), P(), P()),
        out_specs=P(blk, None, None, None, None, "section"),
        check_vma=False,
    )
```

```python
import jax
import jax.numpy as jnp
import numpy as np
from jax import lax
from jax.experimental import pallas as pl
from jax.experimental.pallas import tpu as pltpu
from jax.sharding import Mesh
from jax.sharding import PartitionSpec as P

F = 768
L = 6144
K = 64
CAP = 32
SEG = 8
ROUNDS = 6
LOCAL = 4
HALF = F // 2
Q = L // 4
E = F // 8
ODD = F // 2
EVEN = 128
CLASSES = (0, 4, 2, 6)
LANES = ODD + 4 * EVEN
VMEM = 48 * 1024 * 1024


def angles(steps, freqs):
    return (np.outer(steps, freqs) % L) * (2.0 * np.pi / L)


def odd_bins():
    return np.concatenate([np.arange(1, F, 4), np.arange(3, F, 4)])


def odd_table():
    angle = angles(np.arange(Q), odd_bins())
    sine = np.sin(angle) * np.where(odd_bins() % 4 == 1, 1.0, -1.0)
    return np.concatenate([np.cos(angle), sine], axis=1).astype(np.float32).astype(jnp.bfloat16)


def even_table():
    out = np.zeros((Q // 2, 8, EVEN), np.float32)
    for at, residue in enumerate(CLASSES):
        angle = angles(np.arange(Q // 2), np.arange(residue, F, 8))
        first, second = ((0, 1), (2, 3), (4, 6), (5, 7))[at]
        out[:, first, :E] = np.cos(angle)
        out[:, second, :E] = np.sin(angle) * (-1.0 if residue == 6 else 1.0)
    return out.reshape(Q // 2, 8 * EVEN).astype(jnp.bfloat16)


def tap_tables():
    out = np.zeros((2, K, LANES), np.float32)
    angle = angles(np.arange(K), odd_bins())
    out[:, :, :ODD] = np.cos(angle), np.sin(angle)
    for at, residue in enumerate(CLASSES):
        angle = angles(np.arange(K), np.arange(residue, F, 8))
        start = ODD + at * EVEN
        out[:, :, start : start + E] = np.cos(angle), np.sin(angle)
    return out


def spectra_kernel(
    counts, section, taps, traces, tap_source, odd_source, even_source, out, own, away, x, tap_table, odd, even, spread, y, w, re, im, sems
):
    segs, rows = traces.shape[0], x.shape[0]
    loads = [pltpu.make_async_copy(traces.at[s], x.at[pl.ds(s * CAP, CAP)], sems.at[s]) for s in range(segs)]
    even_load = pltpu.make_async_copy(even_source, even, sems.at[segs])
    odd_load = pltpu.make_async_copy(odd_source, odd, sems.at[segs + 1])
    tap_load = pltpu.make_async_copy(tap_source, tap_table, sems.at[segs + 2])
    for copy in loads:
        copy.start()

    src = lax.broadcasted_iota(jnp.int32, (LANES, F), 0)
    dst = lax.broadcasted_iota(jnp.int32, (LANES, F), 1)
    residue = dst & 7
    place = jnp.where((dst & 3) == 1, dst >> 2, (dst >> 2) + ODD // 2)
    for at, cls in enumerate(CLASSES):
        place = jnp.where(residue == cls, (dst >> 3) + (ODD + at * EVEN), place)
    spread[...] = jnp.where(src == place, 1.0, 0.0).astype(jnp.bfloat16)
    for copy in (even_load, odd_load, tap_load):
        copy.start()

    def tile(t, carry):
        at = pl.ds(pl.multiple_of(t * 16, 16), 16)
        total = jnp.zeros((16, 128), jnp.float32)
        for c in range(L // 128):
            v = x[at, c * 128 : (c + 1) * 128].astype(jnp.float32)
            total = total + v * v
        mean = jnp.sum(total, axis=1, keepdims=True) * (1.0 / L)
        top = jnp.broadcast_to(2.5 * jnp.sqrt(mean + 1e-6), (16, 128))

        def clipped(start):
            v = x[at, start : start + 128].astype(jnp.float32)
            v = jnp.minimum(jnp.maximum(v, -top), top)
            return v.astype(jnp.bfloat16).astype(jnp.float32)

        def keep(ref, n, c, v):
            hi = v.astype(jnp.bfloat16)
            lo = (v - hi.astype(jnp.float32)).astype(jnp.bfloat16)
            ref[2 * n, at, c * 128 : (c + 1) * 128] = hi
            ref[2 * n + 1, at, c * 128 : (c + 1) * 128] = lo

        half = Q // 256
        for c in range(half):
            even_sums = []
            for c_at in (c, c + half):
                x0, x1, x2, x3 = [clipped(q * Q + c_at * 128) for q in range(4)]
                keep(y, 0, c_at, x0 - x2)
                keep(y, 1, c_at, x3 - x1)
                s02, s13 = x0 + x2, x1 + x3
                even_sums.append((s02 + s13, s02 - s13))
            (a0, a2), (b0, b2) = even_sums
            for n, v in enumerate((a0 + b0, a0 - b0, a2, -b2)):
                keep(w, n, c, v)
        return carry

    for s in range(segs):
        loads[s].wait()
        lax.fori_loop(s * CAP // 16, (s + 1) * CAP // 16, tile, 0)

    def product(ref, n, table, lanes):
        a = jnp.dot(ref[2 * n], table[:, lanes], preferred_element_type=jnp.float32)
        b = jnp.dot(ref[2 * n + 1], table[:, lanes], preferred_element_type=jnp.float32)
        return a + b

    even_load.wait()
    for n in range(2):
        p = product(w, n, even, slice(2 * n * EVEN, (2 * n + 2) * EVEN))
        at = slice(ODD + n * EVEN, ODD + (n + 1) * EVEN)
        re[:, at] = p[:, :EVEN]
        im[:, at] = -p[:, EVEN:]

    def paired(p, q, at, width):
        sign = jnp.where(lax.broadcasted_iota(jnp.int32, (1, width), 1) < width // 2, 1.0, -1.0)
        re[:, at] = p[:, :width] + q[:, width:]
        im[:, at] = (q[:, :width] - p[:, width:]) * sign

    lanes = slice(4 * EVEN, 8 * EVEN)
    paired(product(w, 2, even, lanes), product(w, 3, even, lanes), slice(ODD + 2 * EVEN, LANES), 2 * EVEN)
    odd_load.wait()
    lanes = slice(0, 2 * ODD)
    paired(product(y, 0, odd, lanes), product(y, 1, odd, lanes), slice(0, ODD), ODD)

    tap_load.wait()
    square = (K, K)
    same = lax.broadcasted_iota(jnp.int32, square, 0) == lax.broadcasted_iota(jnp.int32, square, 1)
    column = jnp.sum(jnp.where(same, jnp.broadcast_to(taps[...], square), 0.0), axis=1, keepdims=True)
    hr = jnp.sum(tap_table[0] * column, axis=0, keepdims=True)
    hi = -jnp.sum(tap_table[1] * column, axis=0, keepdims=True)
    fr = re[...] * hr - im[...] * hi
    fi = re[...] * hi + im[...] * hr
    power = jnp.sum(fr * fr + fi * fi, axis=1, keepdims=True) * (1.0 / F) + 1e-6
    slot = lax.broadcasted_iota(jnp.int32, (rows, 1), 0) % CAP
    live = jnp.where(slot < counts[0], 1.0, 0.0)
    scale = live / jnp.sqrt(power)
    white = jnp.concatenate([fr * scale, fi * scale], axis=0).astype(jnp.bfloat16)
    ordered = jnp.dot(white, spread[...], preferred_element_type=jnp.float32)
    for half in range(2):
        for seg in range(LOCAL):
            for part in range(2):
                start, piece = part * rows + seg * CAP, seg * 2 + part
                for fg in range(HALF // 128):
                    at = half * HALF + fg * 128
                    block = pltpu.roll(ordered[start : start + CAP, at : at + 128], 16 * piece, 1)
                    out[half, piece, :, fg * 128 : (fg + 1) * 128] = block.astype(jnp.bfloat16)
    for half in range(2):

        @pl.when(section[0] == half)
        def _(half=half):
            own[0] = out[half]
            away[0] = out[1 - half]


def spectra_of(traces, counts, taps, section):
    segs, cap, length = traces.shape
    rows = segs * cap
    far_away = pl.BlockSpec(memory_space=pl.ANY)
    return pl.pallas_call(
        spectra_kernel,
        out_shape=[jax.ShapeDtypeStruct((n, 2 * segs, cap, HALF), jnp.bfloat16) for n in (2, 1, 1)],
        in_specs=[
            pl.BlockSpec(memory_space=pltpu.SMEM),
            pl.BlockSpec(memory_space=pltpu.SMEM),
            pl.BlockSpec(memory_space=pltpu.VMEM),
            far_away,
            far_away,
            far_away,
            far_away,
        ],
        out_specs=[pl.BlockSpec(memory_space=pltpu.VMEM)] * 3,
        scratch_shapes=[
            pltpu.VMEM((rows, length), jnp.bfloat16),
            pltpu.VMEM((2, K, LANES), jnp.float32),
            pltpu.VMEM((Q, 2 * ODD), jnp.bfloat16),
            pltpu.VMEM((Q // 2, 8 * EVEN), jnp.bfloat16),
            pltpu.VMEM((LANES, F), jnp.bfloat16),
            pltpu.VMEM((4, rows, Q), jnp.bfloat16),
            pltpu.VMEM((8, rows, Q // 2), jnp.bfloat16),
            pltpu.VMEM((rows, LANES), jnp.float32),
            pltpu.VMEM((rows, LANES), jnp.float32),
            pltpu.SemaphoreType.DMA((segs + 3,)),
        ],
        compiler_params=pltpu.CompilerParams(vmem_limit_bytes=62 * 1024 * 1024),
        name="spectra",
    )(counts, section, taps.reshape(1, K), traces, tap_tables(), odd_table(), even_table())


def near_round(masks):
    return sum(jnp.where(masks[r] == 1, r, 0) for r in range(ROUNDS))


def far_round(masks, n):
    return n + (n >= near_round(masks)).astype(jnp.int32)


def pick_kernel(masks, z, *refs):
    slabs, (out, held, sems) = (refs[:8], refs[8:16]), refs[16:]
    copies = []
    for n in range(out.shape[1]):
        mask = masks[far_round(masks, n)]
        apart = (jnp.bitwise_xor(z[0], (mask >> 1) & 7) - z[0]) & 7
        across = ((mask >> 4) << 1) | (mask & 1)
        for k in range(8):

            @pl.when(apart == k)
            def _(n=n, k=k, across=across):
                for d in range(out.shape[0]):
                    src = jnp.bitwise_xor(across, d)
                    for h in range(2):
                        held[n, d, h] = slabs[h][k][src]

        copies.append(pltpu.make_async_copy(held.at[n], out.at[:, n], sems.at[n]))
        copies[-1].start()
    for copy in copies:
        copy.wait()


def pick(first, second, masks, z):
    inside = pl.BlockSpec(memory_space=pltpu.VMEM)
    half = (2, CAP // 2, HALF)
    return pl.pallas_call(
        pick_kernel,
        out_shape=jax.ShapeDtypeStruct((16, ROUNDS - 1) + half, jnp.bfloat16),
        in_specs=[pl.BlockSpec(memory_space=pltpu.SMEM)] * 2 + [inside] * 16,
        out_specs=pl.BlockSpec(memory_space=pl.ANY),
        scratch_shapes=[
            pltpu.VMEM((ROUNDS - 1, 16) + half, jnp.bfloat16),
            pltpu.SemaphoreType.DMA((ROUNDS - 1,)),
        ],
        compiler_params=pltpu.CompilerParams(vmem_limit_bytes=8 * 1024 * 1024),
        name="pick",
    )(masks, z, *first, *second)


def place_bits(shape, dtype):
    lane = lax.broadcasted_iota(dtype, shape, 1)
    return [(lane & (16 << b)) != 0 for b in range(3)]


def swirl(tiles, bits):
    held = [tiles[-n % 8] for n in range(8)]
    for b in range(3):
        held = [jnp.where(bits[b], held[(n - (1 << b)) % 8], held[n]) for n in range(8)]
    return held


def fill_weights(own, out, it, fg):
    bits = place_bits((8, 128), jnp.int32)
    row = lax.broadcasted_iota(jnp.int32, (16, 128), 0)
    diagonal = (lax.broadcasted_iota(jnp.int32, (16, 128), 1) & 15) == row
    lanes = pl.ds(pl.multiple_of(fg * 128, 128), 128)
    for h in range(2):
        for piece in range(8):
            block = own[h, piece, it * 16 : (it + 1) * 16, lanes].astype(jnp.float32) * (1.0 / SEG)
            for tile in range(2):
                v = block[tile * 8 : (tile + 1) * 8]
                v = pltpu.roll(pltpu.roll(v, -16 * piece % 128, 1), 0, 1, stride=16, stride_axis=0)
                for b in range(3):
                    v = jnp.where(bits[b], pltpu.roll(v, 8 - (1 << b), 0), v)
                for g in range(8):
                    line = jnp.broadcast_to(v[-g % 8][None], (16, 128))
                    at = h * 128 + (g + piece) % 8 * 16
                    out[fg, g, at : at + 16, tile * 128 : (tile + 1) * 128] = jnp.where(diagonal, line, 0.0).astype(
                        jnp.bfloat16
                    )


GROUPS, HALVES = HALF // 128, CAP // 16


def arrange(left, rounds, r, block):
    bits = place_bits((16, 128), jnp.int16)
    for fg in range(GROUPS):
        for h in range(2):
            for jh in range(2):
                x = [block(p, h, jh, slice(fg * 128, (fg + 1) * 128)) for p in range(8)]
                turned = []
                for p in range(8):
                    other = x[p ^ 1]
                    turned.append(pltpu.roll(other, 16, 1) if p % 2 else -pltpu.roll(other, 112, 1))
                for a, tiles in enumerate((x, turned)):
                    at = pl.ds(pl.multiple_of((a * rounds + r) * CAP + jh * 16, 16), 16)
                    for g, z in enumerate(swirl(tiles, bits)):
                        left[fg, g, at, h * 128 : (h + 1) * 128] = z


def multiply(left, weights, sums, fg):
    for g in range(8):
        sums[fg, g] = jnp.dot(left[fg, g], weights[fg, g], preferred_element_type=jnp.float32).astype(jnp.bfloat16)


def finish(sums, done, rounds, it, fg):
    bits = place_bits((16, 128), jnp.int16)
    for r in range(rounds):
        for a in range(2):
            for jh in range(2):
                row = (a * rounds + r) * CAP + jh * 16
                for tile in range(2):
                    cols = slice(tile * 128, (tile + 1) * 128)
                    turned = swirl([sums[fg, g, row : row + 16, cols] for g in range(8)], bits)
                    for i in range(8):
                        done[r, a, it * 16 + tile * 8 + i, jh * 16 : (jh + 1) * 16, fg * 128 : (fg + 1) * 128] = (
                            pltpu.roll(turned[i], -16 * i % 128, 1)
                        )


def near_kernel(masks, own, sibling, out, weights, left, held, sums, done, sems):
    arrange(left, 1, 0, lambda p, h, jh, lanes: sibling[h, p, jh * 16 : (jh + 1) * 16, lanes])
    copies = []
    for it in range(HALVES):

        def fill(fg, carry, it=it):
            fill_weights(own, held.at[it], it, fg)
            return carry

        lax.fori_loop(0, GROUPS, fill, 0)
        copies.append(pltpu.make_async_copy(held.at[it], weights.at[it], sems.at[it]))
        copies[-1].start()
        for fg in range(GROUPS):
            multiply(left, held.at[it], sums, fg)
            finish(sums, done, 1, it, fg)
    copies.append(pltpu.make_async_copy(done.at[0], out.at[near_round(masks)], sems.at[HALVES]))
    copies[-1].start()
    for copy in copies:
        copy.wait()


def near_of(masks, own, sibling):
    inside = pl.BlockSpec(memory_space=pltpu.VMEM)
    return pl.pallas_call(
        near_kernel,
        out_shape=[
            jax.ShapeDtypeStruct((ROUNDS, 2, CAP, CAP, HALF), jnp.bfloat16),
            jax.ShapeDtypeStruct((HALVES, GROUPS, 8, 256, 256), jnp.bfloat16),
        ],
        in_specs=[pl.BlockSpec(memory_space=pltpu.SMEM), inside, inside],
        out_specs=[pl.BlockSpec(memory_space=pltpu.HBM)] * 2,
        scratch_shapes=[
            pltpu.VMEM((GROUPS, 8, 2 * CAP, 256), jnp.bfloat16),
            pltpu.VMEM((HALVES, GROUPS, 8, 256, 256), jnp.bfloat16),
            pltpu.VMEM((GROUPS, 8, 2 * CAP, 256), jnp.bfloat16),
            pltpu.VMEM((1, 2, CAP, CAP, HALF), jnp.bfloat16),
            pltpu.SemaphoreType.DMA((HALVES + 1,)),
        ],
        compiler_params=pltpu.CompilerParams(vmem_limit_bytes=24 * 1024 * 1024),
        cost_estimate=pl.CostEstimate(flops=400000000, bytes_accessed=9000000, transcendentals=0),
        name="near",
    )(masks, own, sibling)


def far_kernel(masks, partner, weights, kept, out, left, held, sums, done, load_sems, store_sems):
    rounds = ROUNDS - 1
    loads = [
        [
            pltpu.make_async_copy(weights.at[it, fg], held.at[it, fg], load_sems.at[it * GROUPS + fg])
            for fg in range(GROUPS)
        ]
        for it in range(HALVES)
    ]
    for it in range(HALVES):
        for fg in range(GROUPS):
            loads[it][fg].start()

    def arrange_one(r, carry):
        arrange(left, rounds, r, lambda p, h, jh, lanes: partner[2 * p + jh, r, h, :, lanes])
        return carry

    lax.fori_loop(0, rounds, arrange_one, 0)

    def store(it, r):
        part = pl.ds(it * 16, 16)
        return pltpu.make_async_copy(
            done.at[r, :, part], out.at[far_round(masks, r), :, part], store_sems.at[it * rounds + r]
        )

    steps = [(it, fg) for it in range(HALVES) for fg in range(GROUPS)]
    for n, (it, fg) in enumerate(steps + [(HALVES, 0)]):
        if n < len(steps):
            loads[it][fg].wait()
            multiply(left, held.at[it], sums, fg)
        if n > 0:
            last_it, last_fg = steps[n - 1]
            finish(sums, done, rounds, last_it, last_fg)
            if last_fg == GROUPS - 1:
                for r in range(rounds):
                    store(last_it, r).start()

    for it in range(HALVES):
        for r in range(rounds):
            store(it, r).wait()


def far_of(masks, partner, weights, kept):
    rounds = ROUNDS - 1
    rows = 2 * rounds * CAP
    return pl.pallas_call(
        far_kernel,
        out_shape=jax.ShapeDtypeStruct(kept.shape, kept.dtype),
        in_specs=[
            pl.BlockSpec(memory_space=pltpu.SMEM),
            pl.BlockSpec(memory_space=pltpu.VMEM),
            pl.BlockSpec(memory_space=pl.ANY),
            pl.BlockSpec(memory_space=pl.ANY),
        ],
        out_specs=pl.BlockSpec(memory_space=pl.ANY),
        scratch_shapes=[
            pltpu.VMEM((GROUPS, 8, rows, 256), jnp.bfloat16),
            pltpu.VMEM((HALVES, GROUPS, 8, 256, 256), jnp.bfloat16),
            pltpu.VMEM((GROUPS, 8, rows, 256), jnp.bfloat16),
            pltpu.VMEM((rounds,) + kept.shape[1:], jnp.bfloat16),
            pltpu.SemaphoreType.DMA((HALVES * GROUPS,)),
            pltpu.SemaphoreType.DMA((HALVES * rounds,)),
        ],
        input_output_aliases={3: 0},
        compiler_params=pltpu.CompilerParams(vmem_limit_bytes=VMEM),
        name="far",
    )(masks, partner, weights, kept)


def flipped(block, axis):
    return lax.ppermute(block, axis, [(0, 1), (1, 0)])


def around(block, last):
    ring = lax.axis_size("z")

    def shift(held, way):
        return lax.ppermute(held, "z", [(i, (i + way) % ring) for i in range(ring)])

    slabs = [block] * ring
    for step in range(1, ring // 2):
        slabs[-step] = shift(slabs[1 - step], 1)
        slabs[step] = shift(slabs[step - 1], -1)
    slabs[ring // 2] = shift(slabs[(ring // 2 + last) % ring], last)
    return slabs


def shards(traces, counts, taps, masks):
    section = lax.axis_index("section")
    z = lax.axis_index("z")

    white, own, away = spectra_of(traces, counts, taps, section[None])
    pieces = lax.all_to_all(
        white.reshape(32, CAP // 2, HALF), ("section", "yh", "x", "core"), 0, 0, tiled=True
    )
    first, second = around(pieces[:16], 1), around(pieces[16:], -1)

    own, away, _ = lax.optimization_barrier((own, away, pieces))
    other = flipped(away, "section")
    both = jnp.where(section == 0, jnp.concatenate([own, other]), jnp.concatenate([other, own]))
    sibling = flipped(both, "core")

    first, second, both, sibling = lax.optimization_barrier((first, second, both, sibling))
    picked = pick(first, second, masks, z[None])
    picked, both, sibling = lax.optimization_barrier((picked, both, sibling))
    partners = lax.all_to_all(picked.reshape(16, -1, HALF), ("yh", "x", "core"), 0, 0, tiled=True)
    result, weights = near_of(masks, both, sibling)
    return far_of(masks, partners.reshape(picked.shape), weights, result)[None]


def solution(mesh):
    fine = Mesh(mesh.devices.reshape(2, 2, 4, 8, 2), ("section", "yh", "x", "z", "core"))
    blk = ("yh", "x", "z", "core")
    return jax.shard_map(
        shards,
        mesh=fine,
        in_specs=(P("section", blk, None), P(blk), P(), P()),
        out_specs=P(blk, None, None, None, None, "section"),
        check_vma=False,
    )
```

```python
import math

import jax
import jax.numpy as jnp
import numpy as np
from jax import lax
from jax.experimental import pallas as pl
from jax.experimental.pallas import tpu as pltpu
from jax.sharding import Mesh
from jax.sharding import PartitionSpec as P

F = 768
L = 6144
K = 64
CAP = 32
SEG = 8
ROUNDS = 6
LOCAL = 4
HALF = F // 2
Q = L // 4
E = F // 8
ODD = F // 2
EVEN = 128
CLASSES = (0, 4, 2, 6)
LANES = ODD + 4 * EVEN
VMEM = 48 * 1024 * 1024


def angles(steps, freqs):
    return (np.outer(steps, freqs) % L) * (2.0 * np.pi / L)


def odd_bins():
    return np.concatenate([np.arange(1, F, 4), np.arange(3, F, 4)])


def odd_table():
    angle = angles(np.arange(Q), odd_bins())
    sine = np.sin(angle) * np.where(odd_bins() % 4 == 1, 1.0, -1.0)
    return np.concatenate([np.cos(angle), sine], axis=1).astype(np.float32).astype(jnp.bfloat16)


def even_table():
    out = np.zeros((Q // 2, 8, EVEN), np.float32)
    for at, residue in enumerate(CLASSES):
        angle = angles(np.arange(Q // 2), np.arange(residue, F, 8))
        first, second = ((0, 1), (2, 3), (4, 6), (5, 7))[at]
        out[:, first, :E] = np.cos(angle)
        out[:, second, :E] = np.sin(angle) * (-1.0 if residue == 6 else 1.0)
    return out.reshape(Q // 2, 8 * EVEN).astype(jnp.bfloat16)


def tap_tables():
    out = np.zeros((2, K, LANES), np.float32)
    angle = angles(np.arange(K), odd_bins())
    out[:, :, :ODD] = np.cos(angle), np.sin(angle)
    for at, residue in enumerate(CLASSES):
        angle = angles(np.arange(K), np.arange(residue, F, 8))
        start = ODD + at * EVEN
        out[:, :, start : start + E] = np.cos(angle), np.sin(angle)
    return out


def spectra_kernel(
    counts, section, taps, traces, tap_source, odd_source, even_source, out, own, away, x, tap_table, odd, even, spread, y, w, re, im, sems
):
    segs, rows = traces.shape[0], x.shape[0]
    loads = [pltpu.make_async_copy(traces.at[s], x.at[pl.ds(s * CAP, CAP)], sems.at[s]) for s in range(segs)]
    even_load = pltpu.make_async_copy(even_source, even, sems.at[segs])
    odd_load = pltpu.make_async_copy(odd_source, odd, sems.at[segs + 1])
    tap_load = pltpu.make_async_copy(tap_source, tap_table, sems.at[segs + 2])
    for copy in loads:
        copy.start()

    src = lax.broadcasted_iota(jnp.int32, (LANES, F), 0)
    dst = lax.broadcasted_iota(jnp.int32, (LANES, F), 1)
    residue = dst & 7
    place = jnp.where((dst & 3) == 1, dst >> 2, (dst >> 2) + ODD // 2)
    for at, cls in enumerate(CLASSES):
        place = jnp.where(residue == cls, (dst >> 3) + (ODD + at * EVEN), place)
    spread[...] = jnp.where(src == place, 1.0, 0.0).astype(jnp.bfloat16)
    for copy in (even_load, odd_load, tap_load):
        copy.start()

    def tile(t, carry):
        at = pl.ds(pl.multiple_of(t * 16, 16), 16)
        total = jnp.zeros((16, 128), jnp.float32)
        for c in range(L // 128):
            v = x[at, c * 128 : (c + 1) * 128].astype(jnp.float32)
            total = total + v * v
        mean = jnp.sum(total, axis=1, keepdims=True) * (1.0 / L)
        top = jnp.broadcast_to(2.5 * jnp.sqrt(mean + 1e-6), (16, 128))

        def clipped(start):
            v = x[at, start : start + 128].astype(jnp.float32)
            v = jnp.minimum(jnp.maximum(v, -top), top)
            return v.astype(jnp.bfloat16).astype(jnp.float32)

        def keep(ref, n, c, v):
            hi = v.astype(jnp.bfloat16)
            lo = (v - hi.astype(jnp.float32)).astype(jnp.bfloat16)
            ref[2 * n, at, c * 128 : (c + 1) * 128] = hi
            ref[2 * n + 1, at, c * 128 : (c + 1) * 128] = lo

        half = Q // 256
        for c in range(half):
            even_sums = []
            for c_at in (c, c + half):
                x0, x1, x2, x3 = [clipped(q * Q + c_at * 128) for q in range(4)]
                keep(y, 0, c_at, x0 - x2)
                keep(y, 1, c_at, x3 - x1)
                s02, s13 = x0 + x2, x1 + x3
                even_sums.append((s02 + s13, s02 - s13))
            (a0, a2), (b0, b2) = even_sums
            for n, v in enumerate((a0 + b0, a0 - b0, a2, -b2)):
                keep(w, n, c, v)
        return carry

    for s in range(segs):
        loads[s].wait()
        lax.fori_loop(s * CAP // 16, (s + 1) * CAP // 16, tile, 0)

    def product(ref, n, table, lanes):
        a = jnp.dot(ref[2 * n], table[:, lanes], preferred_element_type=jnp.float32)
        b = jnp.dot(ref[2 * n + 1], table[:, lanes], preferred_element_type=jnp.float32)
        return a + b

    even_load.wait()
    for n in range(2):
        p = product(w, n, even, slice(2 * n * EVEN, (2 * n + 2) * EVEN))
        at = slice(ODD + n * EVEN, ODD + (n + 1) * EVEN)
        re[:, at] = p[:, :EVEN]
        im[:, at] = -p[:, EVEN:]

    def paired(p, q, at, width):
        sign = jnp.where(lax.broadcasted_iota(jnp.int32, (1, width), 1) < width // 2, 1.0, -1.0)
        re[:, at] = p[:, :width] + q[:, width:]
        im[:, at] = (q[:, :width] - p[:, width:]) * sign

    lanes = slice(4 * EVEN, 8 * EVEN)
    paired(product(w, 2, even, lanes), product(w, 3, even, lanes), slice(ODD + 2 * EVEN, LANES), 2 * EVEN)
    odd_load.wait()
    lanes = slice(0, 2 * ODD)
    paired(product(y, 0, odd, lanes), product(y, 1, odd, lanes), slice(0, ODD), ODD)

    tap_load.wait()
    square = (K, K)
    same = lax.broadcasted_iota(jnp.int32, square, 0) == lax.broadcasted_iota(jnp.int32, square, 1)
    column = jnp.sum(jnp.where(same, jnp.broadcast_to(taps[...], square), 0.0), axis=1, keepdims=True)
    hr = jnp.sum(tap_table[0] * column, axis=0, keepdims=True)
    hi = -jnp.sum(tap_table[1] * column, axis=0, keepdims=True)
    fr = re[...] * hr - im[...] * hi
    fi = re[...] * hi + im[...] * hr
    power = jnp.sum(fr * fr + fi * fi, axis=1, keepdims=True) * (1.0 / F) + 1e-6
    slot = lax.broadcasted_iota(jnp.int32, (rows, 1), 0) % CAP
    live = jnp.where(slot < counts[0], 1.0, 0.0)
    scale = live / jnp.sqrt(power)
    white = jnp.concatenate([fr * scale, fi * scale], axis=0).astype(jnp.bfloat16)
    ordered = jnp.dot(white, spread[...], preferred_element_type=jnp.float32)
    for half in range(2):
        for seg in range(LOCAL):
            for part in range(2):
                start, piece = part * rows + seg * CAP, seg * 2 + part
                for fg in range(HALF // 128):
                    at = half * HALF + fg * 128
                    block = pltpu.roll(ordered[start : start + CAP, at : at + 128], 16 * piece, 1)
                    out[half, piece, :, fg * 128 : (fg + 1) * 128] = block.astype(jnp.bfloat16)
    for half in range(2):

        @pl.when(section[0] == half)
        def _(half=half):
            own[0] = out[half]
            away[0] = out[1 - half]


def spectra_of(traces, counts, taps, section):
    segs, cap, length = traces.shape
    rows = segs * cap
    far_away = pl.BlockSpec(memory_space=pl.ANY)
    return pl.pallas_call(
        spectra_kernel,
        out_shape=[jax.ShapeDtypeStruct((n, 2 * segs, cap, HALF), jnp.bfloat16) for n in (2, 1, 1)],
        in_specs=[
            pl.BlockSpec(memory_space=pltpu.SMEM),
            pl.BlockSpec(memory_space=pltpu.SMEM),
            pl.BlockSpec(memory_space=pltpu.VMEM),
            far_away,
            far_away,
            far_away,
            far_away,
        ],
        out_specs=[pl.BlockSpec(memory_space=pltpu.VMEM)] * 3,
        scratch_shapes=[
            pltpu.VMEM((rows, length), jnp.bfloat16),
            pltpu.VMEM((2, K, LANES), jnp.float32),
            pltpu.VMEM((Q, 2 * ODD), jnp.bfloat16),
            pltpu.VMEM((Q // 2, 8 * EVEN), jnp.bfloat16),
            pltpu.VMEM((LANES, F), jnp.bfloat16),
            pltpu.VMEM((4, rows, Q), jnp.bfloat16),
            pltpu.VMEM((8, rows, Q // 2), jnp.bfloat16),
            pltpu.VMEM((rows, LANES), jnp.float32),
            pltpu.VMEM((rows, LANES), jnp.float32),
            pltpu.SemaphoreType.DMA((segs + 3,)),
        ],
        compiler_params=pltpu.CompilerParams(vmem_limit_bytes=62 * 1024 * 1024),
        name="spectra",
    )(counts, section, taps.reshape(1, K), traces, tap_tables(), odd_table(), even_table())


FAR = ROUNDS - 2


def round_of(masks, value):
    return sum(jnp.where(masks[r] == value, r, 0) for r in range(ROUNDS))


def far_round(masks, n):
    near, across = round_of(masks, 1), round_of(masks, 127)
    n = n + (n >= jnp.minimum(near, across)).astype(jnp.int32)
    return n + (n >= jnp.maximum(near, across)).astype(jnp.int32)


def pick_kernel(masks, z, *refs):
    slabs, (out, held, sems) = (refs[:8], refs[8:16]), refs[16:]
    copies = []
    for n in range(out.shape[1]):
        mask = masks[far_round(masks, n)]
        apart = (jnp.bitwise_xor(z[0], (mask >> 1) & 7) - z[0]) & 7
        across = ((mask >> 4) << 1) | (mask & 1)
        for k in range(8):

            @pl.when(apart == k)
            def _(n=n, k=k, across=across):
                for d in range(out.shape[0]):
                    src = jnp.bitwise_xor(across, d)
                    for h in range(2):
                        held[n, d, h] = slabs[h][k][src]

        copies.append(pltpu.make_async_copy(held.at[n], out.at[:, n], sems.at[n]))
        copies[-1].start()
    for copy in copies:
        copy.wait()


def pick(first, second, masks, z):
    inside = pl.BlockSpec(memory_space=pltpu.VMEM)
    half = (2, CAP // 2, HALF)
    return pl.pallas_call(
        pick_kernel,
        out_shape=jax.ShapeDtypeStruct((16, FAR) + half, jnp.bfloat16),
        in_specs=[pl.BlockSpec(memory_space=pltpu.SMEM)] * 2 + [inside] * 16,
        out_specs=pl.BlockSpec(memory_space=pl.ANY),
        scratch_shapes=[
            pltpu.VMEM((FAR, 16) + half, jnp.bfloat16),
            pltpu.SemaphoreType.DMA((FAR,)),
        ],
        compiler_params=pltpu.CompilerParams(vmem_limit_bytes=8 * 1024 * 1024),
        name="pick",
    )(masks, z, *first, *second)


def place_bits(shape, dtype):
    lane = lax.broadcasted_iota(dtype, shape, 1)
    return [(lane & (16 << b)) != 0 for b in range(3)]


def swirl(tiles, bits):
    held = [tiles[-n % 8] for n in range(8)]
    for b in range(3):
        held = [jnp.where(bits[b], held[(n - (1 << b)) % 8], held[n]) for n in range(8)]
    return held


def fill_weights(own, out, it, fg):
    bits = place_bits((8, 128), jnp.int32)
    row = lax.broadcasted_iota(jnp.int32, (16, 128), 0)
    diagonal = (lax.broadcasted_iota(jnp.int32, (16, 128), 1) & 15) == row
    lanes = pl.ds(pl.multiple_of(fg * 128, 128), 128)
    for h in range(2):
        for piece in range(8):
            block = own[h, piece, it * 16 : (it + 1) * 16, lanes].astype(jnp.float32) * (1.0 / SEG)
            for tile in range(2):
                v = block[tile * 8 : (tile + 1) * 8]
                v = pltpu.roll(pltpu.roll(v, -16 * piece % 128, 1), 0, 1, stride=16, stride_axis=0)
                for b in range(3):
                    v = jnp.where(bits[b], pltpu.roll(v, 8 - (1 << b), 0), v)
                for g in range(8):
                    line = jnp.broadcast_to(v[-g % 8][None], (16, 128))
                    at = h * 128 + (g + piece) % 8 * 16
                    out[fg, g, at : at + 16, tile * 128 : (tile + 1) * 128] = jnp.where(diagonal, line, 0.0).astype(
                        jnp.bfloat16
                    )


GROUPS, HALVES = HALF // 128, CAP // 16


def arrange(left, rounds, r, block):
    bits = place_bits((16, 128), jnp.int16)
    for fg in range(GROUPS):
        for h in range(2):
            for jh in range(2):
                x = [block(p, h, jh, slice(fg * 128, (fg + 1) * 128)) for p in range(8)]
                turned = []
                for p in range(8):
                    other = x[p ^ 1]
                    turned.append(pltpu.roll(other, 16, 1) if p % 2 else -pltpu.roll(other, 112, 1))
                for a, tiles in enumerate((x, turned)):
                    at = pl.ds(pl.multiple_of((a * rounds + r) * CAP + jh * 16, 16), 16)
                    for g, z in enumerate(swirl(tiles, bits)):
                        left[fg, g, at, h * 128 : (h + 1) * 128] = z


def multiply(left, weights, sums, fg):
    for g in range(8):
        sums[fg, g] = jnp.dot(left[fg, g], weights[fg, g], preferred_element_type=jnp.float32).astype(jnp.bfloat16)


def finish(sums, done, rounds, it, fg):
    bits = place_bits((16, 128), jnp.int16)
    for r in range(rounds):
        for a in range(2):
            for jh in range(2):
                row = (a * rounds + r) * CAP + jh * 16
                for tile in range(2):
                    cols = slice(tile * 128, (tile + 1) * 128)
                    turned = swirl([sums[fg, g, row : row + 16, cols] for g in range(8)], bits)
                    for i in range(8):
                        done[r, a, it * 16 + tile * 8 + i, jh * 16 : (jh + 1) * 16, fg * 128 : (fg + 1) * 128] = (
                            pltpu.roll(turned[i], -16 * i % 128, 1)
                        )


def near_kernel(masks, own, sibling, out, weights, left, held, sums, done, sems):
    arrange(left, 1, 0, lambda p, h, jh, lanes: sibling[h, p, jh * 16 : (jh + 1) * 16, lanes])
    copies = []
    for it in range(HALVES):

        def fill(fg, carry, it=it):
            fill_weights(own, held.at[it], it, fg)
            return carry

        lax.fori_loop(0, GROUPS, fill, 0)
        copies.append(pltpu.make_async_copy(held.at[it], weights.at[it], sems.at[it]))
        copies[-1].start()
        for fg in range(GROUPS):
            multiply(left, held.at[it], sums, fg)
            finish(sums, done, 1, it, fg)
    copies.append(pltpu.make_async_copy(done.at[0], out.at[round_of(masks, 1)], sems.at[HALVES]))
    copies[-1].start()
    for copy in copies:
        copy.wait()


def near_of(masks, own, sibling):
    inside = pl.BlockSpec(memory_space=pltpu.VMEM)
    return pl.pallas_call(
        near_kernel,
        out_shape=[
            jax.ShapeDtypeStruct((ROUNDS, 2, CAP, CAP, HALF), jnp.bfloat16),
            jax.ShapeDtypeStruct((HALVES, GROUPS, 8, 256, 256), jnp.bfloat16),
        ],
        in_specs=[pl.BlockSpec(memory_space=pltpu.SMEM), inside, inside],
        out_specs=[pl.BlockSpec(memory_space=pltpu.HBM)] * 2,
        scratch_shapes=[
            pltpu.VMEM((GROUPS, 8, 2 * CAP, 256), jnp.bfloat16),
            pltpu.VMEM((HALVES, GROUPS, 8, 256, 256), jnp.bfloat16),
            pltpu.VMEM((GROUPS, 8, 2 * CAP, 256), jnp.bfloat16),
            pltpu.VMEM((1, 2, CAP, CAP, HALF), jnp.bfloat16),
            pltpu.SemaphoreType.DMA((HALVES + 1,)),
        ],
        compiler_params=pltpu.CompilerParams(vmem_limit_bytes=24 * 1024 * 1024),
        cost_estimate=pl.CostEstimate(flops=400000000, bytes_accessed=9000000, transcendentals=0),
        name="near",
    )(masks, own, sibling)


def far_kernel(masks, partner, across, weights, kept, out, left, held, sums, done, load_sems, store_sems):
    rounds = FAR + 1
    loads = [
        [
            pltpu.make_async_copy(weights.at[it, fg], held.at[it, fg], load_sems.at[it * GROUPS + fg])
            for fg in range(GROUPS)
        ]
        for it in range(HALVES)
    ]
    for it in range(HALVES):
        for fg in range(GROUPS):
            loads[it][fg].start()

    def arrange_one(r, carry):
        arrange(left, rounds, r, lambda p, h, jh, lanes: partner[2 * p + jh, r, h, :, lanes])
        return carry

    arrange(left, rounds, FAR, lambda p, h, jh, lanes: across[h, p, jh * 16 : (jh + 1) * 16, lanes])
    lax.fori_loop(0, FAR, arrange_one, 0)

    def store(it, r):
        part = pl.ds(it * 16, 16)
        at = far_round(masks, r) if r < FAR else round_of(masks, 127)
        return pltpu.make_async_copy(done.at[r, :, part], out.at[at, :, part], store_sems.at[it * rounds + r])

    steps = [(it, fg) for it in range(HALVES) for fg in range(GROUPS)]
    for n, (it, fg) in enumerate(steps + [(HALVES, 0)]):
        if n < len(steps):
            loads[it][fg].wait()
            multiply(left, held.at[it], sums, fg)
        if n > 0:
            last_it, last_fg = steps[n - 1]
            finish(sums, done, rounds, last_it, last_fg)
            if last_fg == GROUPS - 1:
                for r in range(rounds):
                    store(last_it, r).start()

    for it in range(HALVES):
        for r in range(rounds):
            store(it, r).wait()


def far_of(masks, partner, across, weights, kept):
    rounds = FAR + 1
    rows = 2 * rounds * CAP
    return pl.pallas_call(
        far_kernel,
        out_shape=jax.ShapeDtypeStruct(kept.shape, kept.dtype),
        in_specs=[
            pl.BlockSpec(memory_space=pltpu.SMEM),
            pl.BlockSpec(memory_space=pltpu.VMEM),
            pl.BlockSpec(memory_space=pltpu.VMEM),
            pl.BlockSpec(memory_space=pl.ANY),
            pl.BlockSpec(memory_space=pl.ANY),
        ],
        out_specs=pl.BlockSpec(memory_space=pl.ANY),
        scratch_shapes=[
            pltpu.VMEM((GROUPS, 8, rows, 256), jnp.bfloat16),
            pltpu.VMEM((HALVES, GROUPS, 8, 256, 256), jnp.bfloat16),
            pltpu.VMEM((GROUPS, 8, rows, 256), jnp.bfloat16),
            pltpu.VMEM((rounds,) + kept.shape[1:], jnp.bfloat16),
            pltpu.SemaphoreType.DMA((HALVES * GROUPS,)),
            pltpu.SemaphoreType.DMA((HALVES * rounds,)),
        ],
        input_output_aliases={4: 0},
        compiler_params=pltpu.CompilerParams(vmem_limit_bytes=VMEM),
        name="far",
    )(masks, partner, across, weights, kept)


def turned(block, axes, mask):
    count = math.prod(lax.axis_size(axis) for axis in axes)
    return lax.ppermute(block, axes, [(i, i ^ mask) for i in range(count)])


def around(block, last):
    ring = lax.axis_size("z")

    def shift(held, way):
        return lax.ppermute(held, "z", [(i, (i + way) % ring) for i in range(ring)])

    slabs = [block] * ring
    for step in range(1, ring // 2):
        slabs[-step] = shift(slabs[1 - step], 1)
        slabs[step] = shift(slabs[step - 1], -1)
    slabs[ring // 2] = shift(slabs[(ring // 2 + last) % ring], last)
    return slabs


def shards(traces, counts, taps, masks):
    section = lax.axis_index("section")
    z = lax.axis_index("z")

    white, own, away = spectra_of(traces, counts, taps, section[None])
    pieces = lax.all_to_all(
        white.reshape(32, CAP // 2, HALF), ("section", "yh", "x", "core"), 0, 0, tiled=True
    )
    first, second = around(pieces[:16], 1), around(pieces[16:], -1)

    own, away, _ = lax.optimization_barrier((own, away, pieces))
    other = turned(away, ("section",), 1)
    both = jnp.where(section == 0, jnp.concatenate([own, other]), jnp.concatenate([other, own]))
    sibling = turned(both, ("core",), 1)
    mirror = turned(both, ("yh", "x", "core"), 15)

    first, second, both, sibling, mirror = lax.optimization_barrier((first, second, both, sibling, mirror))
    picked = pick(first, second, masks, z[None])
    picked, both, sibling, mirror = lax.optimization_barrier((picked, both, sibling, mirror))
    partners = lax.all_to_all(picked.reshape(16, -1, HALF), ("yh", "x", "core"), 0, 0, tiled=True)
    across = turned(mirror, ("z",), 7)
    result, weights = near_of(masks, both, sibling)
    return far_of(masks, partners.reshape(picked.shape), across, weights, result)[None]


def solution(mesh):
    fine = Mesh(mesh.devices.reshape(2, 2, 4, 8, 2), ("section", "yh", "x", "z", "core"))
    blk = ("yh", "x", "z", "core")
    return jax.shard_map(
        shards,
        mesh=fine,
        in_specs=(P("section", blk, None), P(blk), P(), P()),
        out_specs=P(blk, None, None, None, None, "section"),
        check_vma=False,
    )
```

```python
import math

import jax
import jax.numpy as jnp
import numpy as np
from jax import lax
from jax.experimental import pallas as pl
from jax.experimental.pallas import tpu as pltpu
from jax.sharding import Mesh
from jax.sharding import PartitionSpec as P

F = 768
L = 6144
K = 64
CAP = 32
SEG = 8
ROUNDS = 6
LOCAL = 4
HALF = F // 2
Q = L // 4
E = F // 8
ODD = F // 2
EVEN = 128
CLASSES = (0, 4, 2, 6)
LANES = ODD + 4 * EVEN
VMEM = 48 * 1024 * 1024


def angles(steps, freqs):
    return (np.outer(steps, freqs) % L) * (2.0 * np.pi / L)


def odd_bins():
    return np.concatenate([np.arange(1, F, 4), np.arange(3, F, 4)])


def odd_table():
    angle = angles(np.arange(Q), odd_bins())
    sine = np.sin(angle) * np.where(odd_bins() % 4 == 1, 1.0, -1.0)
    return np.concatenate([np.cos(angle), sine], axis=1).astype(np.float32).astype(jnp.bfloat16)


def even_table():
    out = np.zeros((Q // 2, 8, EVEN), np.float32)
    for at, residue in enumerate(CLASSES):
        angle = angles(np.arange(Q // 2), np.arange(residue, F, 8))
        first, second = ((0, 1), (2, 3), (4, 6), (5, 7))[at]
        out[:, first, :E] = np.cos(angle)
        out[:, second, :E] = np.sin(angle) * (-1.0 if residue == 6 else 1.0)
    return out.reshape(Q // 2, 8 * EVEN).astype(jnp.bfloat16)


def tap_tables():
    out = np.zeros((2, K, LANES), np.float32)
    angle = angles(np.arange(K), odd_bins())
    out[:, :, :ODD] = np.cos(angle), np.sin(angle)
    for at, residue in enumerate(CLASSES):
        angle = angles(np.arange(K), np.arange(residue, F, 8))
        start = ODD + at * EVEN
        out[:, :, start : start + E] = np.cos(angle), np.sin(angle)
    return out


def spectra_kernel(
    counts, section, taps, traces, tap_source, odd_source, even_source, out, own, away, x, tap_table, odd, even, spread, y, w, re, im, sems
):
    segs, rows = traces.shape[0], x.shape[0]
    loads = [pltpu.make_async_copy(traces.at[s], x.at[pl.ds(s * CAP, CAP)], sems.at[s]) for s in range(segs)]
    even_load = pltpu.make_async_copy(even_source, even, sems.at[segs])
    odd_load = pltpu.make_async_copy(odd_source, odd, sems.at[segs + 1])
    tap_load = pltpu.make_async_copy(tap_source, tap_table, sems.at[segs + 2])
    for copy in loads:
        copy.start()

    src = lax.broadcasted_iota(jnp.int32, (LANES, F), 0)
    dst = lax.broadcasted_iota(jnp.int32, (LANES, F), 1)
    residue = dst & 7
    place = jnp.where((dst & 3) == 1, dst >> 2, (dst >> 2) + ODD // 2)
    for at, cls in enumerate(CLASSES):
        place = jnp.where(residue == cls, (dst >> 3) + (ODD + at * EVEN), place)
    spread[...] = jnp.where(src == place, 1.0, 0.0).astype(jnp.bfloat16)
    for copy in (even_load, odd_load, tap_load):
        copy.start()

    def tile(t, carry):
        at = pl.ds(pl.multiple_of(t * 16, 16), 16)
        total = jnp.zeros((16, 128), jnp.float32)
        for c in range(L // 128):
            v = x[at, c * 128 : (c + 1) * 128].astype(jnp.float32)
            total = total + v * v
        mean = jnp.sum(total, axis=1, keepdims=True) * (1.0 / L)
        top = jnp.broadcast_to(2.5 * jnp.sqrt(mean + 1e-6), (16, 128))

        def clipped(start):
            v = x[at, start : start + 128].astype(jnp.float32)
            v = jnp.minimum(jnp.maximum(v, -top), top)
            return v.astype(jnp.bfloat16).astype(jnp.float32)

        def keep(ref, n, c, v):
            hi = v.astype(jnp.bfloat16)
            lo = (v - hi.astype(jnp.float32)).astype(jnp.bfloat16)
            ref[2 * n, at, c * 128 : (c + 1) * 128] = hi
            ref[2 * n + 1, at, c * 128 : (c + 1) * 128] = lo

        half = Q // 256
        for c in range(half):
            even_sums = []
            for c_at in (c, c + half):
                x0, x1, x2, x3 = [clipped(q * Q + c_at * 128) for q in range(4)]
                keep(y, 0, c_at, x0 - x2)
                keep(y, 1, c_at, x3 - x1)
                s02, s13 = x0 + x2, x1 + x3
                even_sums.append((s02 + s13, s02 - s13))
            (a0, a2), (b0, b2) = even_sums
            for n, v in enumerate((a0 + b0, a0 - b0, a2, -b2)):
                keep(w, n, c, v)
        return carry

    for s in range(segs):
        loads[s].wait()
        lax.fori_loop(s * CAP // 16, (s + 1) * CAP // 16, tile, 0)

    def product(ref, n, table, lanes):
        a = jnp.dot(ref[2 * n], table[:, lanes], preferred_element_type=jnp.float32)
        b = jnp.dot(ref[2 * n + 1], table[:, lanes], preferred_element_type=jnp.float32)
        return a + b

    even_load.wait()
    for n in range(2):
        p = product(w, n, even, slice(2 * n * EVEN, (2 * n + 2) * EVEN))
        at = slice(ODD + n * EVEN, ODD + (n + 1) * EVEN)
        re[:, at] = p[:, :EVEN]
        im[:, at] = -p[:, EVEN:]

    def paired(p, q, at, width):
        sign = jnp.where(lax.broadcasted_iota(jnp.int32, (1, width), 1) < width // 2, 1.0, -1.0)
        re[:, at] = p[:, :width] + q[:, width:]
        im[:, at] = (q[:, :width] - p[:, width:]) * sign

    lanes = slice(4 * EVEN, 8 * EVEN)
    paired(product(w, 2, even, lanes), product(w, 3, even, lanes), slice(ODD + 2 * EVEN, LANES), 2 * EVEN)
    odd_load.wait()
    lanes = slice(0, 2 * ODD)
    paired(product(y, 0, odd, lanes), product(y, 1, odd, lanes), slice(0, ODD), ODD)

    tap_load.wait()
    square = (K, K)
    same = lax.broadcasted_iota(jnp.int32, square, 0) == lax.broadcasted_iota(jnp.int32, square, 1)
    column = jnp.sum(jnp.where(same, jnp.broadcast_to(taps[...], square), 0.0), axis=1, keepdims=True)
    hr = jnp.sum(tap_table[0] * column, axis=0, keepdims=True)
    hi = -jnp.sum(tap_table[1] * column, axis=0, keepdims=True)
    fr = re[...] * hr - im[...] * hi
    fi = re[...] * hi + im[...] * hr
    power = jnp.sum(fr * fr + fi * fi, axis=1, keepdims=True) * (1.0 / F) + 1e-6
    slot = lax.broadcasted_iota(jnp.int32, (rows, 1), 0) % CAP
    live = jnp.where(slot < counts[0], 1.0, 0.0)
    scale = live / jnp.sqrt(power)
    white = jnp.concatenate([fr * scale, fi * scale], axis=0).astype(jnp.bfloat16)
    ordered = jnp.dot(white, spread[...], preferred_element_type=jnp.float32)
    for half in range(2):
        for seg in range(LOCAL):
            for part in range(2):
                start, piece = part * rows + seg * CAP, seg * 2 + part
                for fg in range(HALF // 128):
                    at = half * HALF + fg * 128
                    block = pltpu.roll(ordered[start : start + CAP, at : at + 128], 16 * piece, 1)
                    out[half, piece, :, fg * 128 : (fg + 1) * 128] = block.astype(jnp.bfloat16)
    for half in range(2):

        @pl.when(section[0] == half)
        def _(half=half):
            own[0] = out[half]
            away[0] = out[1 - half]


def spectra_of(traces, counts, taps, section):
    segs, cap, length = traces.shape
    rows = segs * cap
    far_away = pl.BlockSpec(memory_space=pl.ANY)
    return pl.pallas_call(
        spectra_kernel,
        out_shape=[jax.ShapeDtypeStruct((n, 2 * segs, cap, HALF), jnp.bfloat16) for n in (2, 1, 1)],
        in_specs=[
            pl.BlockSpec(memory_space=pltpu.SMEM),
            pl.BlockSpec(memory_space=pltpu.SMEM),
            pl.BlockSpec(memory_space=pltpu.VMEM),
            far_away,
            far_away,
            far_away,
            far_away,
        ],
        out_specs=[pl.BlockSpec(memory_space=pltpu.VMEM)] * 3,
        scratch_shapes=[
            pltpu.VMEM((rows, length), jnp.bfloat16),
            pltpu.VMEM((2, K, LANES), jnp.float32),
            pltpu.VMEM((Q, 2 * ODD), jnp.bfloat16),
            pltpu.VMEM((Q // 2, 8 * EVEN), jnp.bfloat16),
            pltpu.VMEM((LANES, F), jnp.bfloat16),
            pltpu.VMEM((4, rows, Q), jnp.bfloat16),
            pltpu.VMEM((8, rows, Q // 2), jnp.bfloat16),
            pltpu.VMEM((rows, LANES), jnp.float32),
            pltpu.VMEM((rows, LANES), jnp.float32),
            pltpu.SemaphoreType.DMA((segs + 3,)),
        ],
        compiler_params=pltpu.CompilerParams(vmem_limit_bytes=62 * 1024 * 1024),
        name="spectra",
    )(counts, section, taps.reshape(1, K), traces, tap_tables(), odd_table(), even_table())


FAR = ROUNDS - 2


def round_of(masks, value):
    return sum(jnp.where(masks[r] == value, r, 0) for r in range(ROUNDS))


def far_round(masks, n):
    near, across = round_of(masks, 1), round_of(masks, 127)
    n = n + (n >= jnp.minimum(near, across)).astype(jnp.int32)
    return n + (n >= jnp.maximum(near, across)).astype(jnp.int32)


def pick_kernel(masks, z, *refs):
    slabs, (out, held, sems) = (refs[:8], refs[8:16]), refs[16:]
    copies = []
    for n in range(out.shape[1]):
        mask = masks[far_round(masks, n)]
        apart = (jnp.bitwise_xor(z[0], (mask >> 1) & 7) - z[0]) & 7
        across = ((mask >> 4) << 1) | (mask & 1)
        for k in range(8):

            @pl.when(apart == k)
            def _(n=n, k=k, across=across):
                for d in range(out.shape[0]):
                    src = jnp.bitwise_xor(across, d)
                    for h in range(2):
                        held[n, d, h] = slabs[h][k][src]

        copies.append(pltpu.make_async_copy(held.at[n], out.at[:, n], sems.at[n]))
        copies[-1].start()
    for copy in copies:
        copy.wait()


def pick(first, second, masks, z):
    inside = pl.BlockSpec(memory_space=pltpu.VMEM)
    half = (2, CAP // 2, HALF)
    return pl.pallas_call(
        pick_kernel,
        out_shape=jax.ShapeDtypeStruct((16, FAR) + half, jnp.bfloat16),
        in_specs=[pl.BlockSpec(memory_space=pltpu.SMEM)] * 2 + [inside] * 16,
        out_specs=pl.BlockSpec(memory_space=pl.ANY),
        scratch_shapes=[
            pltpu.VMEM((FAR, 16) + half, jnp.bfloat16),
            pltpu.SemaphoreType.DMA((FAR,)),
        ],
        compiler_params=pltpu.CompilerParams(vmem_limit_bytes=8 * 1024 * 1024),
        name="pick",
    )(masks, z, *first, *second)


def place_bits(shape, dtype):
    lane = lax.broadcasted_iota(dtype, shape, 1)
    return [(lane & (16 << b)) != 0 for b in range(3)]


def swirl(tiles, bits):
    held = [tiles[-n % 8] for n in range(8)]
    for b in range(3):
        held = [jnp.where(bits[b], held[(n - (1 << b)) % 8], held[n]) for n in range(8)]
    return held


def fill_weights(own, out, it, fg):
    bits = place_bits((8, 128), jnp.int32)
    row = lax.broadcasted_iota(jnp.int32, (16, 128), 0)
    diagonal = (lax.broadcasted_iota(jnp.int32, (16, 128), 1) & 15) == row
    lanes = pl.ds(pl.multiple_of(fg * 128, 128), 128)
    for h in range(2):
        for piece in range(8):
            block = own[h, piece, it * 16 : (it + 1) * 16, lanes].astype(jnp.float32) * (1.0 / SEG)
            for tile in range(2):
                v = block[tile * 8 : (tile + 1) * 8]
                v = pltpu.roll(pltpu.roll(v, -16 * piece % 128, 1), 0, 1, stride=16, stride_axis=0)
                for b in range(3):
                    v = jnp.where(bits[b], pltpu.roll(v, 8 - (1 << b), 0), v)
                for g in range(8):
                    line = jnp.broadcast_to(v[-g % 8][None], (16, 128))
                    at = h * 128 + (g + piece) % 8 * 16
                    out[fg, g, at : at + 16, tile * 128 : (tile + 1) * 128] = jnp.where(diagonal, line, 0.0).astype(
                        jnp.bfloat16
                    )


GROUPS, HALVES = HALF // 128, CAP // 16


def arrange(left, rounds, r, block):
    bits = place_bits((16, 128), jnp.int16)
    for fg in range(GROUPS):
        for h in range(2):
            for jh in range(2):
                x = [block(p, h, jh, slice(fg * 128, (fg + 1) * 128)) for p in range(8)]
                turned = []
                for p in range(8):
                    other = x[p ^ 1]
                    turned.append(pltpu.roll(other, 16, 1) if p % 2 else -pltpu.roll(other, 112, 1))
                for a, tiles in enumerate((x, turned)):
                    at = pl.ds(pl.multiple_of((a * rounds + r) * CAP + jh * 16, 16), 16)
                    for g, z in enumerate(swirl(tiles, bits)):
                        left[fg, g, at, h * 128 : (h + 1) * 128] = z


def multiply(left, weights, sums, fg):
    for g in range(8):
        sums[fg, g] = jnp.dot(left[fg, g], weights[fg, g], preferred_element_type=jnp.float32).astype(jnp.bfloat16)


def finish(sums, done, rounds, it, fg, after=None):
    bits = place_bits((16, 128), jnp.int16)
    for r in range(rounds):
        for a in range(2):
            for jh in range(2):
                row = (a * rounds + r) * CAP + jh * 16
                for tile in range(2):
                    cols = slice(tile * 128, (tile + 1) * 128)
                    turned = swirl([sums[fg, g, row : row + 16, cols] for g in range(8)], bits)
                    for i in range(8):
                        done[r, a, it * 16 + tile * 8 + i, jh * 16 : (jh + 1) * 16, fg * 128 : (fg + 1) * 128] = (
                            pltpu.roll(turned[i], -16 * i % 128, 1)
                        )
        if after is not None:
            after(r)


def near_kernel(masks, own, sibling, out, weights, left, held, sums, done, sems):
    arrange(left, 1, 0, lambda p, h, jh, lanes: sibling[h, p, jh * 16 : (jh + 1) * 16, lanes])
    copies = []
    for it in range(HALVES):

        def fill(fg, carry, it=it):
            fill_weights(own, held.at[it], it, fg)
            return carry

        lax.fori_loop(0, GROUPS, fill, 0)
        copies.append(pltpu.make_async_copy(held.at[it], weights.at[it], sems.at[it]))
        copies[-1].start()
        for fg in range(GROUPS):
            multiply(left, held.at[it], sums, fg)
            finish(sums, done, 1, it, fg)
    copies.append(pltpu.make_async_copy(done.at[0], out.at[round_of(masks, 1)], sems.at[HALVES]))
    copies[-1].start()
    for copy in copies:
        copy.wait()


def near_of(masks, own, sibling):
    inside = pl.BlockSpec(memory_space=pltpu.VMEM)
    return pl.pallas_call(
        near_kernel,
        out_shape=[
            jax.ShapeDtypeStruct((ROUNDS, 2, CAP, CAP, HALF), jnp.bfloat16),
            jax.ShapeDtypeStruct((HALVES, GROUPS, 8, 256, 256), jnp.bfloat16),
        ],
        in_specs=[pl.BlockSpec(memory_space=pltpu.SMEM), inside, inside],
        out_specs=[pl.BlockSpec(memory_space=pltpu.HBM)] * 2,
        scratch_shapes=[
            pltpu.VMEM((GROUPS, 8, 2 * CAP, 256), jnp.bfloat16),
            pltpu.VMEM((HALVES, GROUPS, 8, 256, 256), jnp.bfloat16),
            pltpu.VMEM((GROUPS, 8, 2 * CAP, 256), jnp.bfloat16),
            pltpu.VMEM((1, 2, CAP, CAP, HALF), jnp.bfloat16),
            pltpu.SemaphoreType.DMA((HALVES + 1,)),
        ],
        compiler_params=pltpu.CompilerParams(vmem_limit_bytes=24 * 1024 * 1024),
        cost_estimate=pl.CostEstimate(flops=400000000, bytes_accessed=9000000, transcendentals=0),
        name="near",
    )(masks, own, sibling)


def far_kernel(masks, partner, across, weights, kept, out, left, held, sums, done, load_sems, store_sems):
    rounds = FAR + 1
    loads = [
        [
            pltpu.make_async_copy(weights.at[it, fg], held.at[it, fg], load_sems.at[it * GROUPS + fg])
            for fg in range(GROUPS)
        ]
        for it in range(HALVES)
    ]
    for it in range(HALVES):
        for fg in range(GROUPS):
            loads[it][fg].start()

    def arrange_one(r, carry):
        arrange(left, rounds, r, lambda p, h, jh, lanes: partner[2 * p + jh, r, h, :, lanes])
        return carry

    arrange(left, rounds, FAR, lambda p, h, jh, lanes: across[h, p, jh * 16 : (jh + 1) * 16, lanes])
    lax.fori_loop(0, FAR, arrange_one, 0)

    def store(it, r):
        part = pl.ds(it * 16, 16)
        at = far_round(masks, r) if r < FAR else round_of(masks, 127)
        return pltpu.make_async_copy(done.at[r, :, part], out.at[at, :, part], store_sems.at[it * rounds + r])

    steps = [(it, fg) for it in range(HALVES) for fg in range(GROUPS)]
    for n, (it, fg) in enumerate(steps + [(HALVES, 0)]):
        if n < len(steps):
            loads[it][fg].wait()
            multiply(left, held.at[it], sums, fg)
        if n > 0:
            last_it, last_fg = steps[n - 1]
            leave = (lambda r, it=last_it: store(it, r).start()) if last_fg == GROUPS - 1 else None
            finish(sums, done, rounds, last_it, last_fg, leave)

    for it in range(HALVES):
        for r in range(rounds):
            store(it, r).wait()


def far_of(masks, partner, across, weights, kept):
    rounds = FAR + 1
    rows = 2 * rounds * CAP
    return pl.pallas_call(
        far_kernel,
        out_shape=jax.ShapeDtypeStruct(kept.shape, kept.dtype),
        in_specs=[
            pl.BlockSpec(memory_space=pltpu.SMEM),
            pl.BlockSpec(memory_space=pltpu.VMEM),
            pl.BlockSpec(memory_space=pltpu.VMEM),
            pl.BlockSpec(memory_space=pl.ANY),
            pl.BlockSpec(memory_space=pl.ANY),
        ],
        out_specs=pl.BlockSpec(memory_space=pl.ANY),
        scratch_shapes=[
            pltpu.VMEM((GROUPS, 8, rows, 256), jnp.bfloat16),
            pltpu.VMEM((HALVES, GROUPS, 8, 256, 256), jnp.bfloat16),
            pltpu.VMEM((GROUPS, 8, rows, 256), jnp.bfloat16),
            pltpu.VMEM((rounds,) + kept.shape[1:], jnp.bfloat16),
            pltpu.SemaphoreType.DMA((HALVES * GROUPS,)),
            pltpu.SemaphoreType.DMA((HALVES * rounds,)),
        ],
        input_output_aliases={4: 0},
        compiler_params=pltpu.CompilerParams(vmem_limit_bytes=VMEM),
        name="far",
    )(masks, partner, across, weights, kept)


def turned(block, axes, mask):
    count = math.prod(lax.axis_size(axis) for axis in axes)
    return lax.ppermute(block, axes, [(i, i ^ mask) for i in range(count)])


def around(chunks):
    ring = lax.axis_size("z")

    def shift(held, way):
        return lax.ppermute(held, "z", [(i, (i + way) % ring) for i in range(ring)])

    slabs = [[chunk] * ring for chunk in chunks]
    for step in range(1, ring // 2):
        for held in slabs:
            held[-step] = shift(held[1 - step], 1)
            held[step] = shift(held[step - 1], -1)
    for n, held in enumerate(slabs):
        way = 1 - 2 * (n % 2)
        held[ring // 2] = shift(held[(ring // 2 + way) % ring], way)
    return slabs


def shards(traces, counts, taps, masks):
    section = lax.axis_index("section")
    z = lax.axis_index("z")

    white, own, away = spectra_of(traces, counts, taps, section[None])
    pieces = lax.all_to_all(
        white.reshape(32, CAP // 2, HALF), ("section", "yh", "x", "core"), 0, 0, tiled=True
    )
    first, second = around((pieces[:16], pieces[16:]))

    own, away, _ = lax.optimization_barrier((own, away, pieces))
    other = turned(away, ("section",), 1)
    both = jnp.where(section == 0, jnp.concatenate([own, other]), jnp.concatenate([other, own]))
    sibling = turned(both, ("core",), 1)
    mirror = turned(both, ("yh", "x", "core"), 15)

    first, second, both, sibling, mirror = lax.optimization_barrier((first, second, both, sibling, mirror))
    picked = pick(first, second, masks, z[None])
    picked, both, sibling, mirror = lax.optimization_barrier((picked, both, sibling, mirror))
    partners = lax.all_to_all(picked.reshape(16, -1, HALF), ("yh", "x", "core"), 0, 0, tiled=True)
    across = turned(mirror, ("z",), 7)
    result, weights = near_of(masks, both, sibling)
    return far_of(masks, partners.reshape(picked.shape), across, weights, result)[None]


def solution(mesh):
    fine = Mesh(mesh.devices.reshape(2, 2, 4, 8, 2), ("section", "yh", "x", "z", "core"))
    blk = ("yh", "x", "z", "core")
    return jax.shard_map(
        shards,
        mesh=fine,
        in_specs=(P("section", blk, None), P(blk), P(), P()),
        out_specs=P(blk, None, None, None, None, "section"),
        check_vma=False,
    )
```
